256 devices in a mesh: rep: 64 (over z, y_lo, x), fsdp: 4 (over y_hi, core).
Axes of the slice: x: 4, y: 4 (y_hi: 2, y_lo: 2; y = y_hi * 2 + y_lo), z: 8, core: 2. Of those that a mesh axis runs over, the one named last changes fastest.
Arguments:
- tokens: bfloat16 [64, 1024, 4096], P('rep', 'fsdp'), as said below
- gain: float32 [64, 4096], P('rep'), may hold values from 0.1 to 1.9
- weight: bfloat16 [64, 1024, 4096], P('rep', 'fsdp'), may hold values from -6 to 6
- momentum: bfloat16 [64, 1024, 4096], P('rep', 'fsdp'), may hold values from -6 to 6
- key_grad: bfloat16 [64, 1024, 1024], P('rep', 'fsdp'), may hold values from -6 to 6
- step: int32 [1], replicated, may hold values from 0 to 999
Outputs:
- projected: bfloat16 [64, 1024, 1024], P('rep', 'fsdp')
- weight_out: bfloat16 [64, 1024, 4096], P('rep', 'fsdp')
- momentum_out: bfloat16 [64, 1024, 4096], P('rep', 'fsdp')
The draws below stay inside these ranges and needn't reach their ends.
Inputs may be any that keep to these rules, and one draw needn't show every extreme that they name: `tokens`: activations entering the layer.
All inputs are finite; a program needn't handle non-finite values.
Results may differ from the reference program's by a relative error of at most 0.0055.
Values may be sent and summed in bfloat16 or wider, within the bound.
No kernel may reach another device: no remote copies, remote signals or barrier semaphores. Data moves between devices by JAX's collectives and lax.ppermute only.
A program may use at most 128 MiB of HBM per device.

```python
import math
import jax
import jax.numpy as jnp
from jax import lax

D = 4096
KVC = 1024
TOKENS = 1024
REP = 64
N_REP = 64


def draw_tokens(key, part):
    key = jax.random.fold_in(key, 11)
    first, second, third = jax.random.split(key, 3)
    row_scale = jnp.exp(jax.random.uniform(second, (REP, TOKENS, 1), minval=0.0, maxval=math.log(10.0)))
    col_scale = jnp.exp(jax.random.uniform(third, (REP, 1, D), minval=0.0, maxval=math.log(10.0)))
    base = jax.random.normal(first, (REP, TOKENS, D))
    return (base * row_scale * col_scale).astype(jnp.bfloat16)


def level_of(rng, shape, pieces, low, largest):
    def one(axis_at, shards_of):
        draws = jax.random.uniform(jax.random.fold_in(jax.random.fold_in(rng, 6), axis_at), (shards_of,), jnp.float32, low / len(pieces), largest / len(pieces))
        return jnp.repeat(jnp.exp(draws), shape[axis_at] // shards_of).reshape((-1,) + (1,) * (len(shape) - axis_at - 1))

    level = one(*pieces[0])
    for cut in pieces[1:]:
        level = level * one(*cut)
    return level


def normal_values(own_key, shape, spread, bound, shards=(), kind=jnp.bfloat16):
    values = spread * jax.random.normal(own_key, shape, jnp.float32)
    if shards:
        values = values * level_of(own_key, shape, shards, -0.22, 0.18)
    return jnp.clip(values, -bound, bound).astype(kind)


def setup_inputs(seed: int = 0) -> dict:
    splits = jax.random.split(jax.random.key(seed), 7)
    tokens = draw_tokens(jax.random.fold_in(splits[6], 71), 0)
    gain = jnp.clip(1.0 + 0.18 * jax.random.normal(splits[1], (REP, D), jnp.float32), 0.1, 1.9)
    weight = normal_values(splits[2], (REP, KVC, D), 1.0, 6.0, ((0, 64), (1, 4)))
    momentum = normal_values(splits[3], (REP, KVC, D), 1.0, 6.0, ((0, 64), (1, 4)))
    key_grad = normal_values(splits[4], (REP, TOKENS, KVC), 1.0, 6.0, ((0, 64), (1, 4)))
    step = jax.random.randint(splits[5], (1,), 0, 1000).astype(jnp.int32)
    return {"tokens": tokens, "gain": gain, "weight": weight, "momentum": momentum, "key_grad": key_grad, "step": step}


epsilon = 1e-05
moment_decay = 0.9

def normalize(tok_rows, gains):
    values = tok_rows.astype(jnp.float32)
    inverse = lax.rsqrt(lax.optimization_barrier(jnp.mean(values * values, axis=-1, keepdims=True)) + epsilon)
    return (values * inverse * gains.astype(jnp.float32)).astype(jnp.bfloat16)

def reference(tokens, gain, weight, momentum, key_grad, step):
    scale = float(D) ** (-0.5)
    learn_rate = 0.05 + 0.1 * step[0].astype(jnp.float32) / 1000.0

    def group(items):
        tok_rows, gains, weights, moments, grads = items
        normed = normalize(tok_rows, gains)
        keys = (jnp.dot(normed, weights.T, preferred_element_type=jnp.float32) * scale).astype(jnp.bfloat16)
        gradient = jnp.dot(grads.T, normed, preferred_element_type=jnp.float32) * scale
        moment_new = moment_decay * moments.astype(jnp.float32) + gradient
        weight_new = weights.astype(jnp.float32) - learn_rate * moment_new
        return (keys, weight_new, moment_new)
    projected, weight_new, moment_new = lax.map(group, (tokens, gain, weight, momentum, key_grad))
    levels = min(5, N_REP.bit_length() - 1)
    selected = (step[0] % levels).astype(jnp.int32)
    partner = jnp.bitwise_xor(jnp.arange(N_REP, dtype=jnp.int32), jnp.left_shift(jnp.int32(1), selected))
    weight_out = ((weight_new + jnp.take(weight_new, partner, axis=0)) * 0.5).astype(jnp.bfloat16)
    momentum_out = ((moment_new + jnp.take(moment_new, partner, axis=0)) * 0.5).astype(jnp.bfloat16)
    return (projected, weight_out, momentum_out)
```

```python
from functools import partial

import jax
import jax.numpy as jnp
from jax import lax
from jax.experimental import pallas as pl
from jax.experimental.pallas import tpu as pltpu
from jax.sharding import PartitionSpec as P

epsilon = 1e-05
moment_decay = 0.9
AXES = ("rep", "fsdp")
PARTS = 2


def norm_kernel(place, tok, gains, k_sib, k_far, k_cross, whole, *parts):
    rows, model = tok.shape
    width = model // len(parts)
    block = k_far.shape[1]
    step = 16

    @pl.loop(0, rows // step)
    def _(i):
        at = pl.ds(pl.multiple_of(i * step, step), step)
        values = tok[at, :].astype(jnp.float32)
        inverse = lax.rsqrt(jnp.mean(values * values, axis=-1, keepdims=True) + epsilon)
        normed = (values * inverse * gains[...]).astype(jnp.bfloat16)
        whole[at, :model] = normed
        for p, part in enumerate(parts):
            part[at, :width] = normed[:, p * width : (p + 1) * width]

    whole[:, model:] = k_sib[...]
    parts[0][:, width : width + block] = k_far[...]
    parts[0][:, width + block :] = k_cross[...]


def normalize(tok, gains, turned, place):
    rows, model = tok.shape
    block = turned.shape[0] // 4
    step = 64
    widths = [model + block] + [model // PARTS + (2 * block if i == 0 else 0) for i in range(PARTS)]

    def k_spec(flip):
        return pl.BlockSpec((step, rows), lambda i, p: ((p[0] ^ flip) * (block // step) + i, 0))

    return pl.pallas_call(
        norm_kernel,
        grid_spec=pltpu.PrefetchScalarGridSpec(
            num_scalar_prefetch=1,
            grid=(rows // step,),
            in_specs=[
                pl.BlockSpec((step, model), lambda i, p: (i, 0)),
                pl.BlockSpec((1, model), lambda i, p: (0, 0)),
                k_spec(1),
                k_spec(2),
                k_spec(3),
            ],
            out_specs=[pl.BlockSpec((step, w), lambda i, p: (i, 0)) for w in widths],
        ),
        out_shape=[jax.ShapeDtypeStruct((rows, w), jnp.bfloat16) for w in widths],
        cost_estimate=pl.CostEstimate(
            flops=4 * rows * model, bytes_accessed=6 * rows * model, transcendentals=rows
        ),
        name="normalize",
    )(place, tok, gains, turned, turned, turned)


def moment_kernel(scale, piece, place, k_own, k_sib, k_far, k_cross, n_own, n_sib, n_far, n_cross, moments, new, sent):
    @pl.loop(0, new.shape[1] // piece)
    def _(i):
        at = pl.ds(pl.multiple_of(i * piece, piece), piece)
        total = None
        for k, n in ((k_own, n_own), (k_sib, n_sib), (k_far, n_far), (k_cross, n_cross)):
            product = jnp.dot(k[...], n[:, at], preferred_element_type=jnp.float32)
            total = product if total is None else total + product
        value = moment_decay * moments[:, at].astype(jnp.float32) + total * scale
        new[:, at] = value
        sent[:, at] = value.astype(jnp.bfloat16)


def moment_part(scale, place, turned, own, sib, far, cross, first, moments, start, columns):
    rows, model = moments.shape
    tokens = own.shape[0]
    tile = 512
    k_specs = [
        pl.BlockSpec((rows, tokens), lambda i, p: (p[0], 0)),
        pl.BlockSpec((rows, tokens), lambda i, p: (0, model // tokens)),
        pl.BlockSpec((rows, tokens), lambda i, p: (0, columns // tokens)),
        pl.BlockSpec((rows, tokens), lambda i, p: (0, columns // tokens + 1)),
    ]
    whole_spec = pl.BlockSpec((tokens, tile), lambda i, p: (0, start // tile + i))
    part_spec = pl.BlockSpec((tokens, tile), lambda i, p: (0, i))
    m_spec = pl.BlockSpec((rows, tile), lambda i, p: (0, start // tile + i))
    o_spec = pl.BlockSpec((rows, tile), lambda i, p: (0, i))
    return pl.pallas_call(
        partial(moment_kernel, scale, 256),
        grid_spec=pltpu.PrefetchScalarGridSpec(
            num_scalar_prefetch=1,
            grid=(columns // tile,),
            in_specs=k_specs + [whole_spec] * 2 + [part_spec] * 2 + [m_spec],
            out_specs=[o_spec, o_spec],
        ),
        out_shape=[
            jax.ShapeDtypeStruct((rows, columns), jnp.float32),
            jax.ShapeDtypeStruct((rows, columns), jnp.bfloat16),
        ],
        cost_estimate=pl.CostEstimate(
            flops=8 * tokens * rows * columns,
            bytes_accessed=(8 * tokens + 8 * rows) * columns,
            transcendentals=0,
        ),
        name="moment_part",
    )(place, turned, sib, *first, own, sib, far, cross, moments)


def project_kernel(scale, per, *refs):
    *sources, weights, out, total = refs
    i = pl.program_id(0)
    rows = weights.shape[0]
    half = len(sources) // 2

    @pl.when(i == 0)
    def _():
        total[...] = jnp.zeros_like(total)

    for part in range(half):

        @pl.when(i // per == part)
        def _(part=part):
            for s in range(2):
                total[:, s * rows : (s + 1) * rows] += lax.dot_general(
                    sources[s * half + part][...],
                    weights[...],
                    (((1,), (1,)), ((), ())),
                    preferred_element_type=jnp.float32,
                )

    @pl.when(i == pl.num_programs(0) - 1)
    def _():
        out[...] = (total[...] * scale).astype(jnp.bfloat16)


def project(scale, first, second, weights):
    tokens = first[0].shape[0]
    rows, model = weights.shape
    tile = 512
    tiles = model // tile
    per = tiles // len(first)
    n_specs = [
        pl.BlockSpec((tokens, tile), lambda i, part=part: (0, jnp.clip(i - part * per, 0, per - 1)))
        for part in range(len(first))
    ]
    return pl.pallas_call(
        partial(project_kernel, scale, per),
        grid=(tiles,),
        in_specs=n_specs * 2 + [pl.BlockSpec((rows, tile), lambda i: (0, i))],
        out_specs=pl.BlockSpec((tokens, 2 * rows), lambda i: (0, 0)),
        out_shape=jax.ShapeDtypeStruct((tokens, 2 * rows), jnp.bfloat16),
        scratch_shapes=[pltpu.VMEM((tokens, 2 * rows), jnp.float32)],
        cost_estimate=pl.CostEstimate(
            flops=4 * tokens * rows * model,
            bytes_accessed=(4 * tokens + 2 * rows) * model,
            transcendentals=0,
        ),
        name="project",
    )(*first, *second, weights)


def place_kernel(place, *refs):
    *blocks, out = refs
    for k, block in enumerate(blocks):

        @pl.when(pl.program_id(0) == k)
        def _(block=block):
            @pl.loop(0, block.shape[0] // 32)
            def _(i):
                at = pl.ds(pl.multiple_of(i * 32, 32), 32)
                out[at, :] = block[at, :]


def place_blocks(place, blocks):
    rows, columns = blocks[0][0].shape
    width = columns // 2
    count = len(blocks)
    return pl.pallas_call(
        place_kernel,
        grid_spec=pltpu.PrefetchScalarGridSpec(
            num_scalar_prefetch=1,
            grid=(count,),
            in_specs=[pl.BlockSpec((rows, width), lambda i, p, half=half: (0, half)) for _, half in blocks],
            out_specs=pl.BlockSpec((rows, width), lambda i, p: (0, p[0] ^ i if count == 4 else i)),
        ),
        out_shape=jax.ShapeDtypeStruct((rows, count * width), jnp.bfloat16),
        cost_estimate=pl.CostEstimate(
            flops=0, bytes_accessed=4 * count * rows * width, transcendentals=0
        ),
        name="place_blocks",
    )(place, *[block for block, _ in blocks])


def average_kernel(start, rate, new, peer, weights, peer_weights, *refs):
    weight_out, moment_out, n_buf, p_buf, w_buf, q_buf, wo_buf, mo_buf, in_sems, out_sems = refs[-10:]
    tiles, rows, tile = n_buf.shape
    step = 32

    def columns(t, start):
        return pl.ds(pl.multiple_of(start + t * tile, tile), tile)

    def takes(t):
        pairs = ((new, 0, n_buf), (peer, 0, p_buf), (weights, start, w_buf), (peer_weights, start, q_buf))
        return [
            pltpu.make_async_copy(ref.at[:, columns(t, at)], buf.at[t], in_sems.at[t, i])
            for i, (ref, at, buf) in enumerate(pairs)
        ]

    def gives(t):
        return [
            pltpu.make_async_copy(buf.at[t], ref.at[:, columns(t, start)], out_sems.at[t, i])
            for i, (buf, ref) in enumerate(((wo_buf, weight_out), (mo_buf, moment_out)))
        ]

    @pl.loop(0, tiles)
    def _(t):
        for copy in takes(t):
            copy.start()

    @pl.loop(0, tiles)
    def _(t):
        for copy in takes(t):
            copy.wait()

        @pl.loop(0, rows // step)
        def _(i):
            at = pl.ds(pl.multiple_of(i * step, step), step)
            moment = (n_buf[t, at, :] + p_buf[t, at, :].astype(jnp.float32)) * 0.5
            weight = w_buf[t, at, :].astype(jnp.float32) + q_buf[t, at, :].astype(jnp.float32)
            wo_buf[t, at, :] = (weight * 0.5 - rate[0] * moment).astype(jnp.bfloat16)
            mo_buf[t, at, :] = moment.astype(jnp.bfloat16)

        for copy in gives(t):
            copy.start()

    @pl.loop(0, tiles)
    def _(t):
        for copy in gives(t):
            copy.wait()


def average_part(rate, new, peer, weights, peer_weights, start, outs):
    rows, model = weights.shape
    columns = new.shape[1]
    tile = 256
    tiles = columns // tile
    hbm = pl.BlockSpec(memory_space=pltpu.HBM)
    shape = jax.ShapeDtypeStruct((rows, model), jnp.bfloat16)
    buf = pltpu.VMEM((tiles, rows, tile), jnp.bfloat16)
    return pl.pallas_call(
        partial(average_kernel, start),
        in_specs=[pl.BlockSpec(memory_space=pltpu.SMEM)] + [hbm] * (4 + len(outs)),
        out_specs=[hbm, hbm],
        out_shape=[shape, shape],
        input_output_aliases={5 + i: i for i in range(len(outs))},
        scratch_shapes=[
            pltpu.VMEM((tiles, rows, tile), jnp.float32),
            *[buf] * 5,
            pltpu.SemaphoreType.DMA((tiles, 4)),
            pltpu.SemaphoreType.DMA((tiles, 2)),
        ],
        compiler_params=pltpu.CompilerParams(vmem_limit_bytes=24 << 20),
        cost_estimate=pl.CostEstimate(
            flops=6 * rows * columns, bytes_accessed=14 * rows * columns, transcendentals=0
        ),
        name="average_part",
    )(rate, new, peer, weights, peer_weights, *outs)


def stage(always, work, *operands):
    def idle(*operands):
        return jax.tree.map(lambda out: jnp.zeros(out.shape, out.dtype), jax.eval_shape(work, *operands))

    return lax.cond(always, work, idle, *operands)


def branch(bit, reps, shards, tok, gains, weights, moments, grads, place, rate, always):
    model = tok.shape[1]
    scale = float(model) ** (-0.5)
    rows = weights.shape[0]
    columns = model // PARTS
    low_bit = 2

    def move(value, rep_flip, shard_flip):
        pairs = [
            (r * shards + s, (r ^ rep_flip) * shards + (s ^ shard_flip))
            for r in range(reps)
            for s in range(shards)
        ]
        return lax.ppermute(value, AXES, pairs)

    flip = 1 << bit
    far_flip = flip if bit == low_bit else 0

    peer_weights = move(weights, flip, 0)
    turned = grads.T
    own, *own_parts = normalize(tok, gains, turned, place)
    far = [move(part, far_flip, 2) for part in own_parts]

    def near_stage(own, weights):
        sib = move(own, 0, 1)
        return sib, project(scale, [own], [sib], weights)

    sib, near = stage(always, near_stage, own, weights)
    far[0], near = lax.optimization_barrier((far[0], near))

    def moment_stage(part, own, sib, here, first, turned, moments):
        there = move(here, 0, 1)
        first = (here, there) if first is None else first
        new, sent = moment_part(
            scale, place, turned, own, sib, here, there, first, moments, part * columns, columns
        )
        return new, sent, there

    new, peer, cross, sent = [], [], [], None
    for part in range(PARTS):
        if part:
            far[part], sent = lax.optimization_barrier((far[part], sent))
        value, sent, there = stage(
            always,
            partial(moment_stage, part),
            own,
            sib,
            far[part],
            (far[0], cross[0]) if part else None,
            turned,
            moments,
        )
        new.append(value)
        cross.append(there)
        if part == 0:
            sent, peer_weights = lax.optimization_barrier((sent, peer_weights))
        peer.append(move(sent, flip, 0))

    def average(part, outs):
        return average_part(rate, new[part], peer[part], weights, peer_weights, part * columns, outs)

    far[0], peer[0], _ = lax.optimization_barrier((far[0], peer[0], sent))
    over = move(project(scale, far, cross, peer_weights if far_flip else weights), far_flip, 2)
    over, outs = lax.optimization_barrier((over, average(0, ())))
    aside = move(place_blocks(place, ((near, 1), (over, 1))), 0, 1)
    projected = place_blocks(place, ((near, 0), (aside, 0), (over, 0), (aside, 1)))
    peer[1], projected = lax.optimization_barrier((peer[1], projected))
    return (projected, *average(1, outs))


def local(tokens, gain, weight, momentum, key_grad, step):
    rate = 0.05 + 0.1 * step.astype(jnp.float32) / 1000.0
    reps, shards = lax.axis_size("rep"), lax.axis_size("fsdp")
    levels = min(5, reps.bit_length() - 1)
    place = lax.axis_index("fsdp").reshape(1)
    branches = [partial(branch, bit, reps, shards) for bit in range(levels)]
    outs = lax.switch(
        step[0] % levels,
        branches,
        tokens[0],
        gain,
        weight[0],
        momentum[0],
        key_grad[0],
        place,
        rate,
        step[0] >= 0,
    )
    return tuple(out[None] for out in outs)


def solution(mesh):
    split = P("rep", "fsdp", None)
    return jax.shard_map(
        local,
        mesh=mesh,
        in_specs=(split, P("rep", None), split, split, split, P()),
        out_specs=(split, split, split),
        check_vma=False,
    )
```

```python
from functools import partial

import jax
import jax.numpy as jnp
from jax import lax
from jax.experimental import pallas as pl
from jax.experimental.pallas import tpu as pltpu
from jax.sharding import PartitionSpec as P

epsilon = 1e-05
moment_decay = 0.9
AXES = ("rep", "fsdp")
PARTS = 2


def norm_kernel(place, tok, gains, k_sib, k_far, k_cross, whole, *parts):
    rows, model = tok.shape
    width = model // len(parts)
    block = k_far.shape[1]
    step = 16

    @pl.loop(0, rows // step)
    def _(i):
        at = pl.ds(pl.multiple_of(i * step, step), step)
        values = tok[at, :].astype(jnp.float32)
        inverse = lax.rsqrt(jnp.mean(values * values, axis=-1, keepdims=True) + epsilon)
        normed = (values * inverse * gains[...]).astype(jnp.bfloat16)
        whole[at, :model] = normed
        for p, part in enumerate(parts):
            part[at, :width] = normed[:, p * width : (p + 1) * width]

    whole[:, model:] = k_sib[...]
    parts[0][:, width : width + block] = k_far[...]
    parts[0][:, width + block :] = k_cross[...]


def normalize(tok, gains, grads, place):
    rows, model = tok.shape
    block = grads.shape[1] // 4
    step = 64
    widths = [model + block] + [model // PARTS + (2 * block if i == 0 else 0) for i in range(PARTS)]

    def k_spec(flip):
        return pl.BlockSpec((step, block), lambda i, p: (i, p[0] ^ flip))

    return pl.pallas_call(
        norm_kernel,
        grid_spec=pltpu.PrefetchScalarGridSpec(
            num_scalar_prefetch=1,
            grid=(rows // step,),
            in_specs=[
                pl.BlockSpec((step, model), lambda i, p: (i, 0)),
                pl.BlockSpec((1, model), lambda i, p: (0, 0)),
                k_spec(1),
                k_spec(2),
                k_spec(3),
            ],
            out_specs=[pl.BlockSpec((step, w), lambda i, p: (i, 0)) for w in widths],
        ),
        out_shape=[jax.ShapeDtypeStruct((rows, w), jnp.bfloat16) for w in widths],
        cost_estimate=pl.CostEstimate(
            flops=4 * rows * model, bytes_accessed=6 * rows * model, transcendentals=rows
        ),
        name="normalize",
    )(place, tok, gains, grads, grads, grads)


def moment_kernel(scale, piece, place, k_own, k_sib, k_far, k_cross, n_own, n_sib, n_far, n_cross, moments, new, sent, keys, turned):
    @pl.when(pl.program_id(0) == 0)
    def _():
        @pl.loop(0, k_own.shape[0] // 32)
        def _(i):
            at = pl.ds(pl.multiple_of(i * 32, 32), 32)
            for s, k in enumerate((k_own, k_sib, k_far, k_cross)):
                keys[s, at, :] = k[at, :]

        @pl.loop(0, 4)
        def _(s):
            turned[s] = keys[s].T

    @pl.loop(0, new.shape[1] // piece)
    def _(i):
        at = pl.ds(pl.multiple_of(i * piece, piece), piece)
        total = None
        for s, n in enumerate((n_own, n_sib, n_far, n_cross)):
            product = jnp.dot(turned[s], n[:, at], preferred_element_type=jnp.float32)
            total = product if total is None else total + product
        value = moment_decay * moments[:, at].astype(jnp.float32) + total * scale
        new[:, at] = value
        sent[:, at] = value.astype(jnp.bfloat16)


def moment_part(scale, place, grads, own, sib, far, cross, first, moments, start, columns):
    rows, model = moments.shape
    tokens = own.shape[0]
    tile = 512
    k_specs = [
        pl.BlockSpec((tokens, rows), lambda i, p: (0, p[0])),
        pl.BlockSpec((tokens, rows), lambda i, p: (0, model // rows)),
        pl.BlockSpec((tokens, rows), lambda i, p: (0, first[0].shape[1] // rows - 2)),
        pl.BlockSpec((tokens, rows), lambda i, p: (0, first[1].shape[1] // rows - 1)),
    ]
    whole_spec = pl.BlockSpec((tokens, tile), lambda i, p: (0, start // tile + i))
    part_spec = pl.BlockSpec((tokens, tile), lambda i, p: (0, i))
    m_spec = pl.BlockSpec((rows, tile), lambda i, p: (0, start // tile + i))
    o_spec = pl.BlockSpec((rows, tile), lambda i, p: (0, i))
    return pl.pallas_call(
        partial(moment_kernel, scale, 256),
        grid_spec=pltpu.PrefetchScalarGridSpec(
            num_scalar_prefetch=1,
            grid=(columns // tile,),
            in_specs=k_specs + [whole_spec] * 2 + [part_spec] * 2 + [m_spec],
            out_specs=[o_spec, o_spec],
            scratch_shapes=[
                pltpu.VMEM((4, tokens, rows), jnp.bfloat16),
                pltpu.VMEM((4, rows, tokens), jnp.bfloat16),
            ],
        ),
        out_shape=[
            jax.ShapeDtypeStruct((rows, columns), jnp.float32),
            jax.ShapeDtypeStruct((rows, columns), jnp.bfloat16),
        ],
        cost_estimate=pl.CostEstimate(
            flops=8 * tokens * rows * columns,
            bytes_accessed=(8 * tokens + 8 * rows) * columns,
            transcendentals=0,
        ),
        name="moment_part",
    )(place, grads, sib, *first, own, sib, far, cross, moments)


def project_kernel(scale, per, *refs):
    *sources, weights, out, total = refs
    i = pl.program_id(0)
    rows = weights.shape[0]
    half = len(sources) // 2

    @pl.when(i == 0)
    def _():
        total[...] = jnp.zeros_like(total)

    for part in range(half):

        @pl.when(i // per == part)
        def _(part=part):
            @pl.loop(0, weights.shape[1] // 256)
            def _(c):
                at = pl.ds(pl.multiple_of(c * 256, 256), 256)
                for s in range(2):
                    total[:, s * rows : (s + 1) * rows] += lax.dot_general(
                        sources[s * half + part][:, at],
                        weights[:, at],
                        (((1,), (1,)), ((), ())),
                        preferred_element_type=jnp.float32,
                    )

    @pl.when(i == pl.num_programs(0) - 1)
    def _():
        out[...] = (total[...] * scale).astype(jnp.bfloat16)


def project(scale, first, second, weights):
    tokens = first[0].shape[0]
    rows, model = weights.shape
    tile = 512
    tiles = model // tile
    per = tiles // len(first)
    n_specs = [
        pl.BlockSpec((tokens, tile), lambda i, part=part: (0, jnp.clip(i - part * per, 0, per - 1)))
        for part in range(len(first))
    ]
    return pl.pallas_call(
        partial(project_kernel, scale, per),
        grid=(tiles,),
        in_specs=n_specs * 2 + [pl.BlockSpec((rows, tile), lambda i: (0, i))],
        out_specs=pl.BlockSpec((tokens, 2 * rows), lambda i: (0, 0)),
        out_shape=jax.ShapeDtypeStruct((tokens, 2 * rows), jnp.bfloat16),
        scratch_shapes=[pltpu.VMEM((tokens, 2 * rows), jnp.float32)],
        cost_estimate=pl.CostEstimate(
            flops=4 * tokens * rows * model,
            bytes_accessed=(4 * tokens + 2 * rows) * model,
            transcendentals=0,
        ),
        name="project",
    )(*first, *second, weights)


def place_kernel(place, *refs):
    *blocks, out = refs
    for k, block in enumerate(blocks):

        @pl.when(pl.program_id(0) == k)
        def _(block=block):
            @pl.loop(0, block.shape[0] // 32)
            def _(i):
                at = pl.ds(pl.multiple_of(i * 32, 32), 32)
                out[at, :] = block[at, :]


def place_blocks(place, blocks):
    rows, columns = blocks[0][0].shape
    width = columns // 2
    count = len(blocks)
    return pl.pallas_call(
        place_kernel,
        grid_spec=pltpu.PrefetchScalarGridSpec(
            num_scalar_prefetch=1,
            grid=(count,),
            in_specs=[pl.BlockSpec((rows, width), lambda i, p, half=half: (0, half)) for _, half in blocks],
            out_specs=pl.BlockSpec((rows, width), lambda i, p: (0, p[0] ^ i if count == 4 else i)),
        ),
        out_shape=jax.ShapeDtypeStruct((rows, count * width), jnp.bfloat16),
        cost_estimate=pl.CostEstimate(
            flops=0, bytes_accessed=4 * count * rows * width, transcendentals=0
        ),
        name="place_blocks",
    )(place, *[block for block, _ in blocks])


def average_kernel(start, rate, new, peer, weights, peer_weights, *refs):
    weight_out, moment_out, n_buf, p_buf, w_buf, q_buf, wo_buf, mo_buf, in_sems, out_sems = refs[-10:]
    tiles, rows, tile = n_buf.shape
    step = 32

    def columns(t, start):
        return pl.ds(pl.multiple_of(start + t * tile, tile), tile)

    def takes(t):
        pairs = ((new, 0, n_buf), (peer, 0, p_buf), (weights, start, w_buf), (peer_weights, start, q_buf))
        return [
            pltpu.make_async_copy(ref.at[:, columns(t, at)], buf.at[t], in_sems.at[t, i])
            for i, (ref, at, buf) in enumerate(pairs)
        ]

    def gives(t):
        return [
            pltpu.make_async_copy(buf.at[t], ref.at[:, columns(t, start)], out_sems.at[t, i])
            for i, (buf, ref) in enumerate(((wo_buf, weight_out), (mo_buf, moment_out)))
        ]

    @pl.loop(0, tiles)
    def _(t):
        for copy in takes(t):
            copy.start()

    @pl.loop(0, tiles)
    def _(t):
        for copy in takes(t):
            copy.wait()

        @pl.loop(0, rows // step)
        def _(i):
            at = pl.ds(pl.multiple_of(i * step, step), step)
            moment = (n_buf[t, at, :] + p_buf[t, at, :].astype(jnp.float32)) * 0.5
            weight = w_buf[t, at, :].astype(jnp.float32) + q_buf[t, at, :].astype(jnp.float32)
            wo_buf[t, at, :] = (weight * 0.5 - rate[0] * moment).astype(jnp.bfloat16)
            mo_buf[t, at, :] = moment.astype(jnp.bfloat16)

        for copy in gives(t):
            copy.start()

    @pl.loop(0, tiles)
    def _(t):
        for copy in gives(t):
            copy.wait()


def average_part(rate, new, peer, weights, peer_weights, start, outs):
    rows, model = weights.shape
    columns = new.shape[1]
    tile = 256
    tiles = columns // tile
    hbm = pl.BlockSpec(memory_space=pltpu.HBM)
    shape = jax.ShapeDtypeStruct((rows, model), jnp.bfloat16)
    buf = pltpu.VMEM((tiles, rows, tile), jnp.bfloat16)
    return pl.pallas_call(
        partial(average_kernel, start),
        in_specs=[pl.BlockSpec(memory_space=pltpu.SMEM)] + [hbm] * (4 + len(outs)),
        out_specs=[hbm, hbm],
        out_shape=[shape, shape],
        input_output_aliases={5 + i: i for i in range(len(outs))},
        scratch_shapes=[
            pltpu.VMEM((tiles, rows, tile), jnp.float32),
            *[buf] * 5,
            pltpu.SemaphoreType.DMA((tiles, 4)),
            pltpu.SemaphoreType.DMA((tiles, 2)),
        ],
        compiler_params=pltpu.CompilerParams(vmem_limit_bytes=24 << 20),
        cost_estimate=pl.CostEstimate(
            flops=6 * rows * columns, bytes_accessed=14 * rows * columns, transcendentals=0
        ),
        name="average_part",
    )(rate, new, peer, weights, peer_weights, *outs)


def stage(always, work, *operands):
    def idle(*operands):
        outs, tree = jax.tree.flatten(jax.eval_shape(work, *operands))
        blank = pl.pallas_call(
            lambda *refs: None,
            out_specs=[pl.BlockSpec(memory_space=pltpu.HBM)] * len(outs),
            out_shape=[jax.ShapeDtypeStruct(out.shape, out.dtype) for out in outs],
            name="blank",
        )()
        return jax.tree.unflatten(tree, blank)

    return lax.cond(always, work, idle, *operands)


def branch(bit, reps, shards, tok, gains, weights, moments, grads, place, rate, always):
    model = tok.shape[1]
    scale = float(model) ** (-0.5)
    rows = weights.shape[0]
    columns = model // PARTS
    low_bit = 2

    def move(value, rep_flip, shard_flip):
        pairs = [
            (r * shards + s, (r ^ rep_flip) * shards + (s ^ shard_flip))
            for r in range(reps)
            for s in range(shards)
        ]
        return lax.ppermute(value, AXES, pairs)

    flip = 1 << bit
    far_flip = flip if bit == low_bit else 0

    peer_weights = move(weights, flip, 0)
    own, *own_parts = normalize(tok, gains, grads, place)
    far = [move(part, far_flip, 2) for part in own_parts]

    def near_stage(own, weights):
        sib = move(own, 0, 1)
        return sib, project(scale, [own], [sib], weights)

    sib, near = stage(always, near_stage, own, weights)
    far[0], near = lax.optimization_barrier((far[0], near))

    def moment_stage(part, own, sib, here, first, grads, moments):
        there = move(here, 0, 1)
        first = (here, there) if first is None else first
        new, sent = moment_part(
            scale, place, grads, own, sib, here, there, first, moments, part * columns, columns
        )
        return new, sent, there

    new, peer, cross, sent = [], [], [], None
    for part in range(PARTS):
        if part:
            far[part], sent = lax.optimization_barrier((far[part], sent))
        first = (far[0], cross[0]) if part else None
        value, sent, there = stage(
            always, partial(moment_stage, part), own, sib, far[part], first, grads, moments
        )
        new.append(value)
        cross.append(there)
        if part == 0:
            sent, peer_weights = lax.optimization_barrier((sent, peer_weights))
        peer.append(move(sent, flip, 0))

    far[0], _ = lax.optimization_barrier((far[0], sent))
    distant = project(scale, far, cross, peer_weights if far_flip else weights)
    distant, peer[0] = lax.optimization_barrier((distant, peer[0]))
    over = move(distant, far_flip, 2)
    over, outs = lax.optimization_barrier(
        (over, average_part(rate, new[0], peer[0], weights, peer_weights, 0, ()))
    )
    aside = move(place_blocks(place, ((near, 1), (over, 1))), 0, 1)
    projected = place_blocks(place, ((near, 0), (aside, 0), (over, 0), (aside, 1)))
    peer[1], projected = lax.optimization_barrier((peer[1], projected))
    return projected, outs, new[1], peer[1], peer_weights


def local(tokens, gain, weight, momentum, key_grad, step):
    rate = 0.05 + 0.1 * step.astype(jnp.float32) / 1000.0
    reps, shards = lax.axis_size("rep"), lax.axis_size("fsdp")
    levels = min(5, reps.bit_length() - 1)
    place = lax.axis_index("fsdp").reshape(1)
    branches = [partial(branch, bit, reps, shards) for bit in range(levels)]
    projected, outs, new, peer, peer_weights = lax.switch(
        step[0] % levels,
        branches,
        tokens[0],
        gain,
        weight[0],
        momentum[0],
        key_grad[0],
        place,
        rate,
        step[0] >= 0,
    )
    outs = average_part(rate, new, peer, weight[0], peer_weights, new.shape[1], outs)
    return tuple(out[None] for out in (projected, *outs))


def solution(mesh):
    split = P("rep", "fsdp", None)
    return jax.shard_map(
        local,
        mesh=mesh,
        in_specs=(split, P("rep", None), split, split, split, P()),
        out_specs=(split, split, split),
        check_vma=False,
    )
```

```python
from functools import partial

import jax
import jax.numpy as jnp
from jax import lax
from jax.experimental import pallas as pl
from jax.experimental.pallas import tpu as pltpu
from jax.sharding import PartitionSpec as P

epsilon = 1e-05
moment_decay = 0.9
AXES = ("rep", "fsdp")
PARTS = 2


def norm_kernel(place, tok, gains, k_far, k_cross, *parts):
    rows, model = tok.shape
    width = model // len(parts)
    block = k_far.shape[1]
    step, piece = 16, 512

    @pl.loop(0, rows // step)
    def _(i):
        at = pl.ds(pl.multiple_of(i * step, step), step)
        squares = jnp.zeros((step, piece), jnp.float32)
        for c in range(0, model, piece):
            values = tok[at, c : c + piece].astype(jnp.float32)
            squares += values * values
        inverse = lax.rsqrt(jnp.sum(squares, axis=-1, keepdims=True) / model + epsilon)
        for c in range(0, model, piece):
            values = tok[at, c : c + piece].astype(jnp.float32)
            normed = (values * inverse * gains[:, c : c + piece]).astype(jnp.bfloat16)
            parts[c // width][at, c % width : c % width + piece] = normed

    parts[0][:, width : width + block] = k_far[...]
    parts[0][:, width + block :] = k_cross[...]


def normalize(tok, gains, grads, place):
    rows, model = tok.shape
    block = grads.shape[1] // 4
    step = 64
    widths = [model // PARTS + (2 * block if i == 0 else 0) for i in range(PARTS)]

    def k_spec(flip):
        return pl.BlockSpec((step, block), lambda i, p: (i, p[0] ^ flip))

    return pl.pallas_call(
        norm_kernel,
        grid_spec=pltpu.PrefetchScalarGridSpec(
            num_scalar_prefetch=1,
            grid=(rows // step,),
            in_specs=[
                pl.BlockSpec((step, model), lambda i, p: (i, 0)),
                pl.BlockSpec((1, model), lambda i, p: (0, 0)),
                k_spec(2),
                k_spec(3),
            ],
            out_specs=[pl.BlockSpec((step, w), lambda i, p: (i, 0)) for w in widths],
        ),
        out_shape=[jax.ShapeDtypeStruct((rows, w), jnp.bfloat16) for w in widths],
        cost_estimate=pl.CostEstimate(
            flops=4 * rows * model, bytes_accessed=5 * rows * model, transcendentals=rows
        ),
        name="normalize",
    )(place, tok, gains, grads, grads)


def pack_kernel(place, *refs):
    *parts, weights, grads, whole, held, sems = refs
    width, model = weights.shape[1] // len(parts), weights.shape[1]
    block = grads.shape[1] // 4
    keys = pl.ds(pl.multiple_of((place[0] ^ 1) * block, block), block)
    pieces = [(part.at[:, :width], p * width, width) for p, part in enumerate(parts)]
    pieces += [(weights, model, model), (grads.at[:, keys], 2 * model, block)]
    copies = [
        pltpu.make_async_copy(ref, held.at[:, at : at + size], sems.at[i])
        for i, (ref, at, size) in enumerate(pieces)
    ]
    for copy in copies:
        copy.start()
    for copy in copies:
        copy.wait()
    out = pltpu.make_async_copy(held, whole, sems.at[len(copies)])
    out.start()
    out.wait()


def pack(parts, weights, grads, place):
    rows, model = weights.shape
    shape = (rows, 2 * model + grads.shape[1] // 4)
    hbm = pl.BlockSpec(memory_space=pltpu.HBM)
    return pl.pallas_call(
        pack_kernel,
        in_specs=[pl.BlockSpec(memory_space=pltpu.SMEM)] + [hbm] * (len(parts) + 2),
        out_specs=hbm,
        out_shape=jax.ShapeDtypeStruct(shape, jnp.bfloat16),
        scratch_shapes=[pltpu.VMEM(shape, jnp.bfloat16), pltpu.SemaphoreType.DMA((len(parts) + 3,))],
        compiler_params=pltpu.CompilerParams(vmem_limit_bytes=16 << 20),
        cost_estimate=pl.CostEstimate(flops=0, bytes_accessed=4 * shape[0] * shape[1], transcendentals=0),
        name="pack",
    )(place, *parts, weights, grads)


def moment_kernel(scale, piece, place, k_own, k_sib, k_far, k_cross, n_own, n_sib, n_far, n_cross, moments, new, sent, keys, turned):
    @pl.when(pl.program_id(0) == 0)
    def _():
        @pl.loop(0, k_own.shape[0] // 32)
        def _(i):
            at = pl.ds(pl.multiple_of(i * 32, 32), 32)
            for s, k in enumerate((k_own, k_sib, k_far, k_cross)):
                keys[s, at, :] = k[at, :]

        @pl.loop(0, 4)
        def _(s):
            turned[s] = keys[s].T

    @pl.loop(0, new.shape[1] // piece)
    def _(i):
        at = pl.ds(pl.multiple_of(i * piece, piece), piece)
        total = None
        for s, n in enumerate((n_own, n_sib, n_far, n_cross)):
            product = jnp.dot(turned[s], n[:, at], preferred_element_type=jnp.float32)
            total = product if total is None else total + product
        value = moment_decay * moments[:, at].astype(jnp.float32) + total * scale
        new[:, at] = value
        sent[:, at] = value.astype(jnp.bfloat16)


def moment_part(scale, place, grads, own, sib, far, cross, first, moments, start, columns):
    rows, model = moments.shape
    tokens = own.shape[0]
    tile = 512
    k_specs = [
        pl.BlockSpec((tokens, rows), lambda i, p: (0, p[0])),
        pl.BlockSpec((tokens, rows), lambda i, p: (0, 2 * model // rows)),
        pl.BlockSpec((tokens, rows), lambda i, p: (0, columns // rows)),
        pl.BlockSpec((tokens, rows), lambda i, p: (0, columns // rows + 1)),
    ]
    whole_spec = pl.BlockSpec((tokens, tile), lambda i, p: (0, start // tile + i))
    part_spec = pl.BlockSpec((tokens, tile), lambda i, p: (0, i))
    m_spec = pl.BlockSpec((rows, tile), lambda i, p: (0, start // tile + i))
    o_spec = pl.BlockSpec((rows, tile), lambda i, p: (0, i))
    return pl.pallas_call(
        partial(moment_kernel, scale, 256),
        grid_spec=pltpu.PrefetchScalarGridSpec(
            num_scalar_prefetch=1,
            grid=(columns // tile,),
            in_specs=k_specs + [whole_spec] * 2 + [part_spec] * 2 + [m_spec],
            out_specs=[o_spec, o_spec],
            scratch_shapes=[
                pltpu.VMEM((4, tokens, rows), jnp.bfloat16),
                pltpu.VMEM((4, rows, tokens), jnp.bfloat16),
            ],
        ),
        out_shape=[
            jax.ShapeDtypeStruct((rows, columns), jnp.float32),
            jax.ShapeDtypeStruct((rows, columns), jnp.bfloat16),
        ],
        cost_estimate=pl.CostEstimate(
            flops=8 * tokens * rows * columns,
            bytes_accessed=(8 * tokens + 8 * rows) * columns,
            transcendentals=0,
        ),
        name="moment_part",
    )(place, grads, sib, *first, own, sib, far, cross, moments)


def project_kernel(scale, per, *refs):
    *sources, own, other, out, total = refs
    i = pl.program_id(0)
    rows = own.shape[0]

    piece, step = 256, 32

    @pl.when(i == 0)
    def _():
        @pl.loop(0, total.shape[0] // step)
        def _(r):
            at = pl.ds(pl.multiple_of(r * step, step), step)
            total[at, :] = jnp.zeros((step, total.shape[1]), jnp.float32)

    for part, source in enumerate(sources):

        @pl.when(i // per == part)
        def _(source=source):
            @pl.loop(0, own.shape[1] // piece)
            def _(c):
                at = pl.ds(pl.multiple_of(c * piece, piece), piece)
                for g, weights in enumerate((own, other)):
                    total[:, g * rows : (g + 1) * rows] += lax.dot_general(
                        source[:, at],
                        weights[:, at],
                        (((1,), (1,)), ((), ())),
                        preferred_element_type=jnp.float32,
                    )

    @pl.when(i == pl.num_programs(0) - 1)
    def _():
        @pl.loop(0, total.shape[0] // step)
        def _(r):
            at = pl.ds(pl.multiple_of(r * step, step), step)
            out[at, :] = (total[at, :] * scale).astype(jnp.bfloat16)


def project(scale, parts, own, other, offset):
    tokens = parts[0].shape[0]
    rows, model = own.shape
    tile = 512
    tiles = model // tile
    per = tiles // len(parts)
    n_specs = [
        pl.BlockSpec((tokens, tile), lambda i, part=part: (0, jnp.clip(i - part * per, 0, per - 1)))
        for part in range(len(parts))
    ]
    return pl.pallas_call(
        partial(project_kernel, scale, per),
        grid=(tiles,),
        in_specs=n_specs
        + [pl.BlockSpec((rows, tile), lambda i, at=at: (0, at // tile + i)) for at in (0, offset)],
        out_specs=pl.BlockSpec((tokens, 2 * rows), lambda i: (0, 0)),
        out_shape=jax.ShapeDtypeStruct((tokens, 2 * rows), jnp.bfloat16),
        scratch_shapes=[pltpu.VMEM((tokens, 2 * rows), jnp.float32)],
        cost_estimate=pl.CostEstimate(
            flops=4 * tokens * rows * model,
            bytes_accessed=(2 * tokens + 4 * rows) * model,
            transcendentals=0,
        ),
        name="project",
    )(*parts, own, other)


def place_kernel(place, *refs):
    *blocks, out = refs
    for k, block in enumerate(blocks):

        @pl.when(pl.program_id(0) == k)
        def _(block=block):
            @pl.loop(0, block.shape[0] // 32)
            def _(i):
                at = pl.ds(pl.multiple_of(i * 32, 32), 32)
                out[at, :] = block[at, :]


def place_blocks(place, blocks):
    rows, columns = blocks[0][0].shape
    width = columns // 2
    count = len(blocks)
    return pl.pallas_call(
        place_kernel,
        grid_spec=pltpu.PrefetchScalarGridSpec(
            num_scalar_prefetch=1,
            grid=(count,),
            in_specs=[pl.BlockSpec((rows, width), lambda i, p, half=half: (0, half)) for _, half in blocks],
            out_specs=pl.BlockSpec((rows, width), lambda i, p: (0, p[0] ^ i)),
        ),
        out_shape=jax.ShapeDtypeStruct((rows, count * width), jnp.bfloat16),
        cost_estimate=pl.CostEstimate(
            flops=0, bytes_accessed=4 * count * rows * width, transcendentals=0
        ),
        name="place_blocks",
    )(place, *[block for block, _ in blocks])


def average_kernel(start, rate, new, peer, weights, peer_weights, *refs):
    weight_out, moment_out, n_buf, p_buf, w_buf, q_buf, wo_buf, mo_buf, in_sems, out_sems = refs[-10:]
    tiles, rows, tile = n_buf.shape
    step = 32

    def columns(t, start):
        return pl.ds(pl.multiple_of(start + t * tile, tile), tile)

    def takes(t):
        pairs = ((new, 0, n_buf), (peer, 0, p_buf), (weights, start, w_buf), (peer_weights, start, q_buf))
        return [
            pltpu.make_async_copy(ref.at[:, columns(t, at)], buf.at[t], in_sems.at[t, i])
            for i, (ref, at, buf) in enumerate(pairs)
        ]

    def gives(t):
        return [
            pltpu.make_async_copy(buf.at[t], ref.at[:, columns(t, start)], out_sems.at[t, i])
            for i, (buf, ref) in enumerate(((wo_buf, weight_out), (mo_buf, moment_out)))
        ]

    @pl.loop(0, tiles)
    def _(t):
        for copy in takes(t):
            copy.start()

    @pl.loop(0, tiles)
    def _(t):
        for copy in takes(t):
            copy.wait()

        @pl.loop(0, rows // step)
        def _(i):
            at = pl.ds(pl.multiple_of(i * step, step), step)
            moment = (n_buf[t, at, :] + p_buf[t, at, :].astype(jnp.float32)) * 0.5
            weight = w_buf[t, at, :].astype(jnp.float32) + q_buf[t, at, :].astype(jnp.float32)
            wo_buf[t, at, :] = (weight * 0.5 - rate[0] * moment).astype(jnp.bfloat16)
            mo_buf[t, at, :] = moment.astype(jnp.bfloat16)

        for copy in gives(t):
            copy.start()

    @pl.loop(0, tiles)
    def _(t):
        for copy in gives(t):
            copy.wait()


def average_part(rate, new, peer, weights, peer_weights, start, outs):
    rows, model = weights.shape
    columns = new.shape[1]
    tile = 256
    tiles = columns // tile
    hbm = pl.BlockSpec(memory_space=pltpu.HBM)
    shape = jax.ShapeDtypeStruct((rows, model), jnp.bfloat16)
    buf = pltpu.VMEM((tiles, rows, tile), jnp.bfloat16)
    return pl.pallas_call(
        partial(average_kernel, start),
        in_specs=[pl.BlockSpec(memory_space=pltpu.SMEM)] + [hbm] * (4 + len(outs)),
        out_specs=[hbm, hbm],
        out_shape=[shape, shape],
        input_output_aliases={5 + i: i for i in range(len(outs))},
        scratch_shapes=[
            pltpu.VMEM((tiles, rows, tile), jnp.float32),
            *[buf] * 5,
            pltpu.SemaphoreType.DMA((tiles, 4)),
            pltpu.SemaphoreType.DMA((tiles, 2)),
        ],
        compiler_params=pltpu.CompilerParams(vmem_limit_bytes=24 << 20),
        cost_estimate=pl.CostEstimate(
            flops=6 * rows * columns, bytes_accessed=14 * rows * columns, transcendentals=0
        ),
        name="average_part",
    )(rate, new, peer, weights, peer_weights, *outs)


def stage(always, work, *operands):
    def idle(*operands):
        outs, tree = jax.tree.flatten(jax.eval_shape(work, *operands))
        blank = pl.pallas_call(
            lambda *refs: None,
            out_specs=[pl.BlockSpec(memory_space=pltpu.HBM)] * len(outs),
            out_shape=[jax.ShapeDtypeStruct(out.shape, out.dtype) for out in outs],
            name="blank",
        )()
        return jax.tree.unflatten(tree, blank)

    return lax.cond(always, work, idle, *operands)


def branch(bit, reps, shards, tok, gains, weights, moments, grads, place, rate, always):
    model = tok.shape[1]
    scale = float(model) ** (-0.5)
    rows = weights.shape[0]
    columns = model // PARTS
    low_bit = 2

    def move(value, rep_flip, shard_flip):
        pairs = [
            (r * shards + s, (r ^ rep_flip) * shards + (s ^ shard_flip))
            for r in range(reps)
            for s in range(shards)
        ]
        return lax.ppermute(value, AXES, pairs)

    flip = 1 << bit
    far_flip = flip if bit == low_bit else 0

    peer_weights = move(weights, flip, 0)
    own_parts = normalize(tok, gains, grads, place)
    far = [move(part, far_flip, 2) for part in own_parts]

    def near_stage(parts, weights, grads):
        own = pack(parts, weights, grads, place)
        sib = move(own, 0, 1)
        return own, sib, project(scale, [own], weights, sib, model)

    own, sib, near = stage(always, near_stage, own_parts, weights, grads)
    far[0], near = lax.optimization_barrier((far[0], near))

    def moment_stage(part, own, sib, here, first, grads, moments, share):
        there = move(here, 0, 1)
        shared = [move(value, 0, 1) for value in share]
        first = (here, there) if first is None else first
        new, sent = moment_part(
            scale, place, grads, own, sib, here, there, first, moments, part * columns, columns
        )
        return new, sent, there, shared

    new, peer, cross, sent, shared = [], [], [], None, []
    for part in range(PARTS):
        if part:
            far[part], sent = lax.optimization_barrier((far[part], sent))
        first = (far[0], cross[0]) if part else None
        share = [peer_weights] if part and far_flip else []
        value, sent, there, shared = stage(
            always, partial(moment_stage, part), own, sib, far[part], first, grads, moments, share
        )
        new.append(value)
        cross.append(there)
        if part == 0:
            sent, peer_weights = lax.optimization_barrier((sent, peer_weights))
        peer.append(move(sent, flip, 0))

    def average(part, outs):
        return average_part(rate, new[part], peer[part], weights, peer_weights, part * columns, outs)

    far[0], _ = lax.optimization_barrier((far[0], sent))
    if far_flip:
        distant = project(scale, far, peer_weights, shared[0], 0)
    else:
        distant = project(scale, far, weights, sib, model)
    distant, peer[0] = lax.optimization_barrier((distant, peer[0]))
    over = move(distant, far_flip, 2)
    over, outs = lax.optimization_barrier((over, average(0, ())))
    projected = place_blocks(place, ((near, 0), (near, 1), (over, 0), (over, 1)))
    peer[1], projected = lax.optimization_barrier((peer[1], projected))
    return (projected, *average(1, outs))


def local(tokens, gain, weight, momentum, key_grad, step):
    rate = 0.05 + 0.1 * step.astype(jnp.float32) / 1000.0
    reps, shards = lax.axis_size("rep"), lax.axis_size("fsdp")
    levels = min(5, reps.bit_length() - 1)
    place = lax.axis_index("fsdp").reshape(1)
    branches = [partial(branch, bit, reps, shards) for bit in range(levels)]
    outs = lax.switch(
        step[0] % levels,
        branches,
        tokens[0],
        gain,
        weight[0],
        momentum[0],
        key_grad[0],
        place,
        rate,
        step[0] >= 0,
    )
    return tuple(out[None] for out in outs)


def solution(mesh):
    split = P("rep", "fsdp", None)
    return jax.shard_map(
        local,
        mesh=mesh,
        in_specs=(split, P("rep", None), split, split, split, P()),
        out_specs=(split, split, split),
        check_vma=False,
    )
```

```python
from functools import partial

import jax
import jax.numpy as jnp
from jax import lax
from jax.experimental import pallas as pl
from jax.experimental.pallas import tpu as pltpu
from jax.sharding import PartitionSpec as P

epsilon = 1e-05
moment_decay = 0.9
AXES = ("rep", "fsdp")
PARTS = 2


def norm_kernel(place, tok, gains, k_far, k_cross, *parts):
    rows, model = tok.shape
    width = model // len(parts)
    block = k_far.shape[1]
    step, piece = 16, 512

    @pl.loop(0, rows // step)
    def _(i):
        at = pl.ds(pl.multiple_of(i * step, step), step)
        squares = jnp.zeros((step, piece), jnp.float32)
        for c in range(0, model, piece):
            values = tok[at, c : c + piece].astype(jnp.float32)
            squares += values * values
        inverse = lax.rsqrt(jnp.sum(squares, axis=-1, keepdims=True) / model + epsilon)
        for c in range(0, model, piece):
            values = tok[at, c : c + piece].astype(jnp.float32)
            normed = (values * inverse * gains[:, c : c + piece]).astype(jnp.bfloat16)
            parts[c // width][at, c % width : c % width + piece] = normed

    parts[0][:, width : width + block] = k_far[...]
    parts[0][:, width + block :] = k_cross[...]


def normalize(tok, gains, grads, place):
    rows, model = tok.shape
    block = grads.shape[1] // 4
    step = 64
    widths = [model // PARTS + (2 * block if i == 0 else 0) for i in range(PARTS)]

    def k_spec(flip):
        return pl.BlockSpec((step, block), lambda i, p: (i, p[0] ^ flip))

    return pl.pallas_call(
        norm_kernel,
        grid_spec=pltpu.PrefetchScalarGridSpec(
            num_scalar_prefetch=1,
            grid=(rows // step,),
            in_specs=[
                pl.BlockSpec((step, model), lambda i, p: (i, 0)),
                pl.BlockSpec((1, model), lambda i, p: (0, 0)),
                k_spec(2),
                k_spec(3),
            ],
            out_specs=[pl.BlockSpec((step, w), lambda i, p: (i, 0)) for w in widths],
        ),
        out_shape=[jax.ShapeDtypeStruct((rows, w), jnp.bfloat16) for w in widths],
        cost_estimate=pl.CostEstimate(
            flops=4 * rows * model, bytes_accessed=5 * rows * model, transcendentals=rows
        ),
        name="normalize",
    )(place, tok, gains, grads, grads)


def pack_kernel(place, *refs):
    *parts, weights, grads, whole, held, sems = refs
    width, model = weights.shape[1] // len(parts), weights.shape[1]
    block = grads.shape[1] // 4
    keys = pl.ds(pl.multiple_of((place[0] ^ 1) * block, block), block)
    pieces = [(part.at[:, :width], p * width, width) for p, part in enumerate(parts)]
    pieces += [(weights, model, model), (grads.at[:, keys], 2 * model, block)]
    copies = [
        pltpu.make_async_copy(ref, held.at[:, at : at + size], sems.at[i])
        for i, (ref, at, size) in enumerate(pieces)
    ]
    for copy in copies:
        copy.start()
    for copy in copies:
        copy.wait()
    out = pltpu.make_async_copy(held, whole, sems.at[len(copies)])
    out.start()
    out.wait()


def pack(parts, weights, grads, place):
    rows, model = weights.shape
    shape = (rows, 2 * model + grads.shape[1] // 4)
    hbm = pl.BlockSpec(memory_space=pltpu.HBM)
    return pl.pallas_call(
        pack_kernel,
        in_specs=[pl.BlockSpec(memory_space=pltpu.SMEM)] + [hbm] * (len(parts) + 2),
        out_specs=hbm,
        out_shape=jax.ShapeDtypeStruct(shape, jnp.bfloat16),
        scratch_shapes=[pltpu.VMEM(shape, jnp.bfloat16), pltpu.SemaphoreType.DMA((len(parts) + 3,))],
        compiler_params=pltpu.CompilerParams(vmem_limit_bytes=16 << 20),
        cost_estimate=pl.CostEstimate(flops=0, bytes_accessed=4 * shape[0] * shape[1], transcendentals=0),
        name="pack",
    )(place, *parts, weights, grads)


def moment_kernel(scale, piece, place, k_own, k_sib, k_far, k_cross, n_own, n_sib, n_far, n_cross, moments, new, sent, keys, turned):
    @pl.when(pl.program_id(0) == 0)
    def _():
        @pl.loop(0, k_own.shape[0] // 32)
        def _(i):
            at = pl.ds(pl.multiple_of(i * 32, 32), 32)
            for s, k in enumerate((k_own, k_sib, k_far, k_cross)):
                keys[s, at, :] = k[at, :]

        @pl.loop(0, 4)
        def _(s):
            turned[s] = keys[s].T

    @pl.loop(0, new.shape[1] // piece)
    def _(i):
        at = pl.ds(pl.multiple_of(i * piece, piece), piece)
        total = None
        for s, n in enumerate((n_own, n_sib, n_far, n_cross)):
            product = jnp.dot(turned[s], n[:, at], preferred_element_type=jnp.float32)
            total = product if total is None else total + product
        value = moment_decay * moments[:, at].astype(jnp.float32) + total * scale
        new[:, at] = value
        sent[:, at] = value.astype(jnp.bfloat16)


def moment_part(scale, place, grads, own, sib, far, cross, first, moments, start, columns):
    rows, model = moments.shape
    tokens = own.shape[0]
    tile = 1024
    k_specs = [
        pl.BlockSpec((tokens, rows), lambda i, p: (0, p[0])),
        pl.BlockSpec((tokens, rows), lambda i, p: (0, 2 * model // rows)),
        pl.BlockSpec((tokens, rows), lambda i, p: (0, columns // rows)),
        pl.BlockSpec((tokens, rows), lambda i, p: (0, columns // rows + 1)),
    ]
    whole_spec = pl.BlockSpec((tokens, tile), lambda i, p: (0, start // tile + i))
    part_spec = pl.BlockSpec((tokens, tile), lambda i, p: (0, i))
    m_spec = pl.BlockSpec((rows, tile), lambda i, p: (0, start // tile + i))
    o_spec = pl.BlockSpec((rows, tile), lambda i, p: (0, i))
    return pl.pallas_call(
        partial(moment_kernel, scale, 256),
        grid_spec=pltpu.PrefetchScalarGridSpec(
            num_scalar_prefetch=1,
            grid=(columns // tile,),
            in_specs=k_specs + [whole_spec] * 2 + [part_spec] * 2 + [m_spec],
            out_specs=[o_spec, o_spec],
            scratch_shapes=[
                pltpu.VMEM((4, tokens, rows), jnp.bfloat16),
                pltpu.VMEM((4, rows, tokens), jnp.bfloat16),
            ],
        ),
        out_shape=[
            jax.ShapeDtypeStruct((rows, columns), jnp.float32),
            jax.ShapeDtypeStruct((rows, columns), jnp.bfloat16),
        ],
        cost_estimate=pl.CostEstimate(
            flops=8 * tokens * rows * columns,
            bytes_accessed=(8 * tokens + 8 * rows) * columns,
            transcendentals=0,
        ),
        name="moment_part",
    )(place, grads, sib, *first, own, sib, far, cross, moments)


def project_kernel(scale, per, *refs):
    *sources, own, other, out, total = refs
    i = pl.program_id(0)
    rows = own.shape[0]

    piece, step = 256, 32

    @pl.when(i == 0)
    def _():
        @pl.loop(0, total.shape[0] // step)
        def _(r):
            at = pl.ds(pl.multiple_of(r * step, step), step)
            total[at, :] = jnp.zeros((step, total.shape[1]), jnp.float32)

    for part, source in enumerate(sources):

        @pl.when(i // per == part)
        def _(source=source):
            @pl.loop(0, own.shape[1] // piece)
            def _(c):
                at = pl.ds(pl.multiple_of(c * piece, piece), piece)
                for g, weights in enumerate((own, other)):
                    total[:, g * rows : (g + 1) * rows] += lax.dot_general(
                        source[:, at],
                        weights[:, at],
                        (((1,), (1,)), ((), ())),
                        preferred_element_type=jnp.float32,
                    )

    @pl.when(i == pl.num_programs(0) - 1)
    def _():
        @pl.loop(0, total.shape[0] // step)
        def _(r):
            at = pl.ds(pl.multiple_of(r * step, step), step)
            out[at, :] = (total[at, :] * scale).astype(jnp.bfloat16)


def project(scale, parts, own, other, offset):
    tokens = parts[0].shape[0]
    rows, model = own.shape
    tile = 512
    tiles = model // tile
    per = tiles // len(parts)
    n_specs = [
        pl.BlockSpec((tokens, tile), lambda i, part=part: (0, jnp.clip(i - part * per, 0, per - 1)))
        for part in range(len(parts))
    ]
    return pl.pallas_call(
        partial(project_kernel, scale, per),
        grid=(tiles,),
        in_specs=n_specs
        + [pl.BlockSpec((rows, tile), lambda i, at=at: (0, at // tile + i)) for at in (0, offset)],
        out_specs=pl.BlockSpec((tokens, 2 * rows), lambda i: (0, 0)),
        out_shape=jax.ShapeDtypeStruct((tokens, 2 * rows), jnp.bfloat16),
        scratch_shapes=[pltpu.VMEM((tokens, 2 * rows), jnp.float32)],
        cost_estimate=pl.CostEstimate(
            flops=4 * tokens * rows * model,
            bytes_accessed=(2 * tokens + 4 * rows) * model,
            transcendentals=0,
        ),
        name="project",
    )(*parts, own, other)


def place_kernel(place, *refs):
    *blocks, out = refs
    for k, block in enumerate(blocks):

        @pl.when(pl.program_id(0) == k)
        def _(block=block):
            @pl.loop(0, block.shape[0] // 32)
            def _(i):
                at = pl.ds(pl.multiple_of(i * 32, 32), 32)
                out[at, :] = block[at, :]


def place_blocks(place, blocks):
    rows, columns = blocks[0][0].shape
    width = columns // 2
    count = len(blocks)
    return pl.pallas_call(
        place_kernel,
        grid_spec=pltpu.PrefetchScalarGridSpec(
            num_scalar_prefetch=1,
            grid=(count,),
            in_specs=[pl.BlockSpec((rows, width), lambda i, p, half=half: (0, half)) for _, half in blocks],
            out_specs=pl.BlockSpec((rows, width), lambda i, p: (0, p[0] ^ i)),
        ),
        out_shape=jax.ShapeDtypeStruct((rows, count * width), jnp.bfloat16),
        cost_estimate=pl.CostEstimate(
            flops=0, bytes_accessed=4 * count * rows * width, transcendentals=0
        ),
        name="place_blocks",
    )(place, *[block for block, _ in blocks])


def average_kernel(start, rate, new, peer, weights, peer_weights, *refs):
    weight_out, moment_out, n_buf, p_buf, w_buf, q_buf, wo_buf, mo_buf, in_sems, out_sems = refs[-10:]
    tiles, rows, tile = n_buf.shape
    step = 64

    def columns(t, start):
        return pl.ds(pl.multiple_of(start + t * tile, tile), tile)

    def takes(t):
        pairs = ((new, 0, n_buf), (peer, 0, p_buf), (weights, start, w_buf), (peer_weights, start, q_buf))
        return [
            pltpu.make_async_copy(ref.at[:, columns(t, at)], buf.at[t], in_sems.at[t, i])
            for i, (ref, at, buf) in enumerate(pairs)
        ]

    def gives(t):
        return [
            pltpu.make_async_copy(buf.at[t], ref.at[:, columns(t, start)], out_sems.at[t, i])
            for i, (buf, ref) in enumerate(((wo_buf, weight_out), (mo_buf, moment_out)))
        ]

    @pl.loop(0, tiles)
    def _(t):
        for copy in takes(t):
            copy.start()

    @pl.loop(0, tiles)
    def _(t):
        for copy in takes(t):
            copy.wait()

        @pl.loop(0, rows // step)
        def _(i):
            at = pl.ds(pl.multiple_of(i * step, step), step)
            moment = (n_buf[t, at, :] + p_buf[t, at, :].astype(jnp.float32)) * 0.5
            weight = w_buf[t, at, :].astype(jnp.float32) + q_buf[t, at, :].astype(jnp.float32)
            wo_buf[t, at, :] = (weight * 0.5 - rate[0] * moment).astype(jnp.bfloat16)
            mo_buf[t, at, :] = moment.astype(jnp.bfloat16)

        for copy in gives(t):
            copy.start()

    @pl.loop(0, tiles)
    def _(t):
        for copy in gives(t):
            copy.wait()


def average_part(rate, new, peer, weights, peer_weights, start, outs):
    rows, model = weights.shape
    columns = new.shape[1]
    tile = 256
    tiles = columns // tile
    hbm = pl.BlockSpec(memory_space=pltpu.HBM)
    shape = jax.ShapeDtypeStruct((rows, model), jnp.bfloat16)
    buf = pltpu.VMEM((tiles, rows, tile), jnp.bfloat16)
    return pl.pallas_call(
        partial(average_kernel, start),
        in_specs=[pl.BlockSpec(memory_space=pltpu.SMEM)] + [hbm] * (4 + len(outs)),
        out_specs=[hbm, hbm],
        out_shape=[shape, shape],
        input_output_aliases={5 + i: i for i in range(len(outs))},
        scratch_shapes=[
            pltpu.VMEM((tiles, rows, tile), jnp.float32),
            *[buf] * 5,
            pltpu.SemaphoreType.DMA((tiles, 4)),
            pltpu.SemaphoreType.DMA((tiles, 2)),
        ],
        compiler_params=pltpu.CompilerParams(vmem_limit_bytes=24 << 20),
        cost_estimate=pl.CostEstimate(
            flops=6 * rows * columns, bytes_accessed=14 * rows * columns, transcendentals=0
        ),
        name="average_part",
    )(rate, new, peer, weights, peer_weights, *outs)


def stage(always, work, *operands):
    def idle(*operands):
        outs, tree = jax.tree.flatten(jax.eval_shape(work, *operands))
        blank = pl.pallas_call(
            lambda *refs: None,
            out_specs=[pl.BlockSpec(memory_space=pltpu.HBM)] * len(outs),
            out_shape=[jax.ShapeDtypeStruct(out.shape, out.dtype) for out in outs],
            name="blank",
        )()
        return jax.tree.unflatten(tree, blank)

    return lax.cond(always, work, idle, *operands)


def branch(bit, reps, shards, tok, gains, weights, moments, grads, place, rate, always):
    model = tok.shape[1]
    scale = float(model) ** (-0.5)
    rows = weights.shape[0]
    columns = model // PARTS
    low_bit = 2

    def move(value, rep_flip, shard_flip):
        pairs = [
            (r * shards + s, (r ^ rep_flip) * shards + (s ^ shard_flip))
            for r in range(reps)
            for s in range(shards)
        ]
        return lax.ppermute(value, AXES, pairs)

    flip = 1 << bit
    far_flip = flip if bit == low_bit else 0

    peer_weights = move(weights, flip, 0)
    own_parts = normalize(tok, gains, grads, place)
    far = [move(part, far_flip, 2) for part in own_parts]

    def near_stage(parts, weights, grads):
        own = pack(parts, weights, grads, place)
        sib = move(own, 0, 1)
        return own, sib, project(scale, [own], weights, sib, model)

    own, sib, near = stage(always, near_stage, own_parts, weights, grads)
    far[0], near = lax.optimization_barrier((far[0], near))

    def moment_stage(part, own, sib, here, first, grads, moments, share):
        there = move(here, 0, 1)
        shared = [move(value, 0, 1) for value in share]
        first = (here, there) if first is None else first
        new, sent = moment_part(
            scale, place, grads, own, sib, here, there, first, moments, part * columns, columns
        )
        return new, sent, there, shared

    new, peer, cross, sent, shared = [], [], [], None, []
    for part in range(PARTS):
        if part:
            far[part], sent = lax.optimization_barrier((far[part], sent))
        first = (far[0], cross[0]) if part else None
        share = [peer_weights] if part and far_flip else []
        value, sent, there, shared = stage(
            always, partial(moment_stage, part), own, sib, far[part], first, grads, moments, share
        )
        new.append(value)
        cross.append(there)
        if part == 0:
            sent, peer_weights = lax.optimization_barrier((sent, peer_weights))
        peer.append(move(sent, flip, 0))

    def average(part, outs):
        return average_part(rate, new[part], peer[part], weights, peer_weights, part * columns, outs)

    far[0], _ = lax.optimization_barrier((far[0], sent))
    if far_flip:
        distant = project(scale, far, peer_weights, shared[0], 0)
    else:
        distant = project(scale, far, weights, sib, model)
    distant, peer[0] = lax.optimization_barrier((distant, peer[0]))
    over = move(distant, far_flip, 2)
    over, outs = lax.optimization_barrier((over, average(0, ())))
    projected = place_blocks(place, ((near, 0), (near, 1), (over, 0), (over, 1)))
    peer[1], projected = lax.optimization_barrier((peer[1], projected))
    return (projected, *average(1, outs))


def local(tokens, gain, weight, momentum, key_grad, step):
    rate = 0.05 + 0.1 * step.astype(jnp.float32) / 1000.0
    reps, shards = lax.axis_size("rep"), lax.axis_size("fsdp")
    levels = min(5, reps.bit_length() - 1)
    place = lax.axis_index("fsdp").reshape(1)
    branches = [partial(branch, bit, reps, shards) for bit in range(levels)]
    outs = lax.switch(
        lax.rem(step[0], levels),
        branches,
        tokens[0],
        gain,
        weight[0],
        momentum[0],
        key_grad[0],
        place,
        rate,
        step[0] >= 0,
    )
    return tuple(out[None] for out in outs)


def solution(mesh):
    split = P("rep", "fsdp", None)
    return jax.shard_map(
        local,
        mesh=mesh,
        in_specs=(split, P("rep", None), split, split, split, P()),
        out_specs=(split, split, split),
        check_vma=False,
    )
```

```python
from functools import partial

import jax
import jax.numpy as jnp
from jax import lax
from jax.experimental import pallas as pl
from jax.experimental.pallas import tpu as pltpu
from jax.sharding import PartitionSpec as P

epsilon = 1e-05
moment_decay = 0.9
AXES = ("rep", "fsdp")
PARTS = 2


def norm_kernel(place, tok, gains, k_far, k_cross, *parts):
    rows, model = tok.shape
    width = model // len(parts)
    block = k_far.shape[1]
    step, piece = 16, 512

    @pl.loop(0, rows // step)
    def _(i):
        at = pl.ds(pl.multiple_of(i * step, step), step)
        squares = jnp.zeros((step, piece), jnp.float32)
        for c in range(0, model, piece):
            values = tok[at, c : c + piece].astype(jnp.float32)
            squares += values * values
        inverse = lax.rsqrt(jnp.sum(squares, axis=-1, keepdims=True) / model + epsilon)
        for c in range(0, model, piece):
            values = tok[at, c : c + piece].astype(jnp.float32)
            normed = (values * inverse * gains[:, c : c + piece]).astype(jnp.bfloat16)
            parts[c // width][at, c % width : c % width + piece] = normed

    parts[0][:, width : width + block] = k_far[...]
    parts[0][:, width + block :] = k_cross[...]


def normalize(tok, gains, grads, place):
    rows, model = tok.shape
    block = grads.shape[1] // 4
    step = 64
    widths = [model // PARTS + (2 * block if i == 0 else 0) for i in range(PARTS)]

    def k_spec(flip):
        return pl.BlockSpec((step, block), lambda i, p: (i, p[0] ^ flip))

    return pl.pallas_call(
        norm_kernel,
        grid_spec=pltpu.PrefetchScalarGridSpec(
            num_scalar_prefetch=1,
            grid=(rows // step,),
            in_specs=[
                pl.BlockSpec((step, model), lambda i, p: (i, 0)),
                pl.BlockSpec((1, model), lambda i, p: (0, 0)),
                k_spec(2),
                k_spec(3),
            ],
            out_specs=[pl.BlockSpec((step, w), lambda i, p: (i, 0)) for w in widths],
        ),
        out_shape=[jax.ShapeDtypeStruct((rows, w), jnp.bfloat16) for w in widths],
        cost_estimate=pl.CostEstimate(
            flops=4 * rows * model, bytes_accessed=5 * rows * model, transcendentals=rows
        ),
        name="normalize",
    )(place, tok, gains, grads, grads)


def pack_kernel(place, *refs):
    *parts, weights, grads, whole, held, sems = refs
    width, model = weights.shape[1] // len(parts), weights.shape[1]
    block = grads.shape[1] // 4
    keys = pl.ds(pl.multiple_of((place[0] ^ 1) * block, block), block)
    pieces = [(part.at[:, :width], p * width, width) for p, part in enumerate(parts)]
    pieces += [(weights, model, model), (grads.at[:, keys], 2 * model, block)]
    copies = [
        pltpu.make_async_copy(ref, held.at[:, at : at + size], sems.at[i])
        for i, (ref, at, size) in enumerate(pieces)
    ]
    for copy in copies:
        copy.start()
    for copy in copies:
        copy.wait()
    out = pltpu.make_async_copy(held, whole, sems.at[len(copies)])
    out.start()
    out.wait()


def pack(parts, weights, grads, place):
    rows, model = weights.shape
    shape = (rows, 2 * model + grads.shape[1] // 4)
    hbm = pl.BlockSpec(memory_space=pltpu.HBM)
    return pl.pallas_call(
        pack_kernel,
        in_specs=[pl.BlockSpec(memory_space=pltpu.SMEM)] + [hbm] * (len(parts) + 2),
        out_specs=hbm,
        out_shape=jax.ShapeDtypeStruct(shape, jnp.bfloat16),
        scratch_shapes=[pltpu.VMEM(shape, jnp.bfloat16), pltpu.SemaphoreType.DMA((len(parts) + 3,))],
        compiler_params=pltpu.CompilerParams(vmem_limit_bytes=16 << 20),
        cost_estimate=pl.CostEstimate(flops=0, bytes_accessed=4 * shape[0] * shape[1], transcendentals=0),
        name="pack",
    )(place, *parts, weights, grads)


def moment_kernel(scale, piece, place, k_own, k_sib, k_far, k_cross, n_own, n_sib, n_far, n_cross, moments, new, sent, keys, turned):
    @pl.when(pl.program_id(0) == 0)
    def _():
        @pl.loop(0, k_own.shape[0] // 32)
        def _(i):
            at = pl.ds(pl.multiple_of(i * 32, 32), 32)
            for s, k in enumerate((k_own, k_sib, k_far, k_cross)):
                keys[s, at, :] = k[at, :]

        @pl.loop(0, 4)
        def _(s):
            turned[s] = keys[s].T

    @pl.loop(0, new.shape[1] // piece)
    def _(i):
        at = pl.ds(pl.multiple_of(i * piece, piece), piece)
        total = None
        for s, n in enumerate((n_own, n_sib, n_far, n_cross)):
            product = jnp.dot(turned[s], n[:, at], preferred_element_type=jnp.float32)
            total = product if total is None else total + product
        value = moment_decay * moments[:, at].astype(jnp.float32) + total * scale
        new[:, at] = value
        sent[:, at] = value.astype(jnp.bfloat16)


def moment_part(scale, place, grads, own, sib, far, cross, first, moments, start, columns):
    rows, model = moments.shape
    tokens = own.shape[0]
    tile = 1024
    k_specs = [
        pl.BlockSpec((tokens, rows), lambda i, p: (0, p[0])),
        pl.BlockSpec((tokens, rows), lambda i, p: (0, 2 * model // rows)),
        pl.BlockSpec((tokens, rows), lambda i, p: (0, columns // rows)),
        pl.BlockSpec((tokens, rows), lambda i, p: (0, columns // rows + 1)),
    ]
    whole_spec = pl.BlockSpec((tokens, tile), lambda i, p: (0, start // tile + i))
    part_spec = pl.BlockSpec((tokens, tile), lambda i, p: (0, i))
    m_spec = pl.BlockSpec((rows, tile), lambda i, p: (0, start // tile + i))
    o_spec = pl.BlockSpec((rows, tile), lambda i, p: (0, i))
    return pl.pallas_call(
        partial(moment_kernel, scale, 256),
        grid_spec=pltpu.PrefetchScalarGridSpec(
            num_scalar_prefetch=1,
            grid=(columns // tile,),
            in_specs=k_specs + [whole_spec] * 2 + [part_spec] * 2 + [m_spec],
            out_specs=[o_spec, o_spec],
            scratch_shapes=[
                pltpu.VMEM((4, tokens, rows), jnp.bfloat16),
                pltpu.VMEM((4, rows, tokens), jnp.bfloat16),
            ],
        ),
        out_shape=[
            jax.ShapeDtypeStruct((rows, columns), jnp.float32),
            jax.ShapeDtypeStruct((rows, columns), jnp.bfloat16),
        ],
        cost_estimate=pl.CostEstimate(
            flops=8 * tokens * rows * columns,
            bytes_accessed=(8 * tokens + 8 * rows) * columns,
            transcendentals=0,
        ),
        name="moment_part",
    )(place, grads, sib, *first, own, sib, far, cross, moments)


def project_kernel(scale, per, *refs):
    *sources, own, other, out, total = refs
    i = pl.program_id(0)
    rows = own.shape[0]

    piece, step = 256, 32

    @pl.when(i == 0)
    def _():
        @pl.loop(0, total.shape[0] // step)
        def _(r):
            at = pl.ds(pl.multiple_of(r * step, step), step)
            total[at, :] = jnp.zeros((step, total.shape[1]), jnp.float32)

    for part, source in enumerate(sources):

        @pl.when(i // per == part)
        def _(source=source):
            @pl.loop(0, own.shape[1] // piece)
            def _(c):
                at = pl.ds(pl.multiple_of(c * piece, piece), piece)
                for g, weights in enumerate((own, other)):
                    total[:, g * rows : (g + 1) * rows] += lax.dot_general(
                        source[:, at],
                        weights[:, at],
                        (((1,), (1,)), ((), ())),
                        preferred_element_type=jnp.float32,
                    )

    @pl.when(i == pl.num_programs(0) - 1)
    def _():
        @pl.loop(0, total.shape[0] // step)
        def _(r):
            at = pl.ds(pl.multiple_of(r * step, step), step)
            out[at, :] = (total[at, :] * scale).astype(jnp.bfloat16)


def project(scale, parts, own, other, offset):
    tokens = parts[0].shape[0]
    rows, model = own.shape
    tile = 512
    tiles = model // tile
    per = tiles // len(parts)
    n_specs = [
        pl.BlockSpec((tokens, tile), lambda i, part=part: (0, jnp.clip(i - part * per, 0, per - 1)))
        for part in range(len(parts))
    ]
    return pl.pallas_call(
        partial(project_kernel, scale, per),
        grid=(tiles,),
        in_specs=n_specs
        + [pl.BlockSpec((rows, tile), lambda i, at=at: (0, at // tile + i)) for at in (0, offset)],
        out_specs=pl.BlockSpec((tokens, 2 * rows), lambda i: (0, 0)),
        out_shape=jax.ShapeDtypeStruct((tokens, 2 * rows), jnp.bfloat16),
        scratch_shapes=[pltpu.VMEM((tokens, 2 * rows), jnp.float32)],
        cost_estimate=pl.CostEstimate(
            flops=4 * tokens * rows * model,
            bytes_accessed=(2 * tokens + 4 * rows) * model,
            transcendentals=0,
        ),
        name="project",
    )(*parts, own, other)


def place_kernel(place, *refs):
    *blocks, out = refs
    for k, block in enumerate(blocks):

        @pl.when(pl.program_id(0) == k)
        def _(block=block):
            @pl.loop(0, block.shape[0] // 32)
            def _(i):
                at = pl.ds(pl.multiple_of(i * 32, 32), 32)
                out[at, :] = block[at, :]


def place_blocks(place, blocks):
    rows, columns = blocks[0][0].shape
    width = columns // 2
    count = len(blocks)
    return pl.pallas_call(
        place_kernel,
        grid_spec=pltpu.PrefetchScalarGridSpec(
            num_scalar_prefetch=1,
            grid=(count,),
            in_specs=[pl.BlockSpec((rows, width), lambda i, p, half=half: (0, half)) for _, half in blocks],
            out_specs=pl.BlockSpec((rows, width), lambda i, p: (0, p[0] ^ i)),
        ),
        out_shape=jax.ShapeDtypeStruct((rows, count * width), jnp.bfloat16),
        cost_estimate=pl.CostEstimate(
            flops=0, bytes_accessed=4 * count * rows * width, transcendentals=0
        ),
        name="place_blocks",
    )(place, *[block for block, _ in blocks])


def average_kernel(start, rate, new, peer, weights, peer_weights, *refs):
    weight_out, moment_out, n_buf, p_buf, w_buf, q_buf, wo_buf, mo_buf, in_sems, out_sems = refs[-10:]
    tiles, rows, tile = n_buf.shape
    step = 64

    def columns(t, start):
        return pl.ds(pl.multiple_of(start + t * tile, tile), tile)

    def takes(t):
        pairs = ((new, 0, n_buf), (peer, 0, p_buf), (weights, start, w_buf), (peer_weights, start, q_buf))
        return [
            pltpu.make_async_copy(ref.at[:, columns(t, at)], buf.at[t], in_sems.at[t, i])
            for i, (ref, at, buf) in enumerate(pairs)
        ]

    def gives(t):
        return [
            pltpu.make_async_copy(buf.at[t], ref.at[:, columns(t, start)], out_sems.at[t, i])
            for i, (buf, ref) in enumerate(((wo_buf, weight_out), (mo_buf, moment_out)))
        ]

    @pl.loop(0, tiles)
    def _(t):
        for copy in takes(t):
            copy.start()

    @pl.loop(0, tiles)
    def _(t):
        for copy in takes(t):
            copy.wait()

        @pl.loop(0, rows // step)
        def _(i):
            at = pl.ds(pl.multiple_of(i * step, step), step)
            moment = (n_buf[t, at, :] + p_buf[t, at, :].astype(jnp.float32)) * 0.5
            weight = w_buf[t, at, :].astype(jnp.float32) + q_buf[t, at, :].astype(jnp.float32)
            wo_buf[t, at, :] = (weight * 0.5 - rate[0] * moment).astype(jnp.bfloat16)
            mo_buf[t, at, :] = moment.astype(jnp.bfloat16)

        for copy in gives(t):
            copy.start()

    @pl.loop(0, tiles)
    def _(t):
        for copy in gives(t):
            copy.wait()


def average_part(rate, new, peer, weights, peer_weights, start, outs):
    rows, model = weights.shape
    columns = new.shape[1]
    tile = 512
    tiles = columns // tile
    hbm = pl.BlockSpec(memory_space=pltpu.HBM)
    shape = jax.ShapeDtypeStruct((rows, model), jnp.bfloat16)
    buf = pltpu.VMEM((tiles, rows, tile), jnp.bfloat16)
    return pl.pallas_call(
        partial(average_kernel, start),
        in_specs=[pl.BlockSpec(memory_space=pltpu.SMEM)] + [hbm] * (4 + len(outs)),
        out_specs=[hbm, hbm],
        out_shape=[shape, shape],
        input_output_aliases={5 + i: i for i in range(len(outs))},
        scratch_shapes=[
            pltpu.VMEM((tiles, rows, tile), jnp.float32),
            *[buf] * 5,
            pltpu.SemaphoreType.DMA((tiles, 4)),
            pltpu.SemaphoreType.DMA((tiles, 2)),
        ],
        compiler_params=pltpu.CompilerParams(vmem_limit_bytes=24 << 20),
        cost_estimate=pl.CostEstimate(
            flops=6 * rows * columns, bytes_accessed=14 * rows * columns, transcendentals=0
        ),
        name="average_part",
    )(rate, new, peer, weights, peer_weights, *outs)


def stage(always, work, *operands):
    def idle(*operands):
        outs, tree = jax.tree.flatten(jax.eval_shape(work, *operands))
        blank = pl.pallas_call(
            lambda *refs: None,
            out_specs=[pl.BlockSpec(memory_space=pltpu.HBM)] * len(outs),
            out_shape=[jax.ShapeDtypeStruct(out.shape, out.dtype) for out in outs],
            name="blank",
        )()
        return jax.tree.unflatten(tree, blank)

    return lax.cond(always, work, idle, *operands)


def branch(bit, reps, shards, tok, gains, weights, moments, grads, place, rate, always):
    model = tok.shape[1]
    scale = float(model) ** (-0.5)
    rows = weights.shape[0]
    columns = model // PARTS
    low_bit = 2

    def move(value, rep_flip, shard_flip):
        pairs = [
            (r * shards + s, (r ^ rep_flip) * shards + (s ^ shard_flip))
            for r in range(reps)
            for s in range(shards)
        ]
        return lax.ppermute(value, AXES, pairs)

    flip = 1 << bit
    far_flip = flip if bit == low_bit else 0

    peer_weights = move(weights, flip, 0)
    own_parts = normalize(tok, gains, grads, place)
    far = [move(part, far_flip, 2) for part in own_parts]

    def near_stage(parts, weights, grads):
        own = pack(parts, weights, grads, place)
        sib = move(own, 0, 1)
        return own, sib, project(scale, [own], weights, sib, model)

    own, sib, near = stage(always, near_stage, own_parts, weights, grads)
    far[0], near = lax.optimization_barrier((far[0], near))

    def moment_stage(part, own, sib, here, first, grads, moments, share):
        there = move(here, 0, 1)
        shared = [move(value, 0, 1) for value in share]
        first = (here, there) if first is None else first
        new, sent = moment_part(
            scale, place, grads, own, sib, here, there, first, moments, part * columns, columns
        )
        return new, sent, there, shared

    new, peer, cross, sent, shared = [], [], [], None, []
    for part in range(PARTS):
        if part:
            far[part], sent = lax.optimization_barrier((far[part], sent))
        first = (far[0], cross[0]) if part else None
        share = [peer_weights] if part and far_flip else []
        value, sent, there, shared = stage(
            always, partial(moment_stage, part), own, sib, far[part], first, grads, moments, share
        )
        new.append(value)
        cross.append(there)
        if part == 0:
            sent, peer_weights = lax.optimization_barrier((sent, peer_weights))
        peer.append(move(sent, flip, 0))

    def average(part, outs):
        return average_part(rate, new[part], peer[part], weights, peer_weights, part * columns, outs)

    far[0], _ = lax.optimization_barrier((far[0], sent))
    if far_flip:
        distant = project(scale, far, peer_weights, shared[0], 0)
    else:
        distant = project(scale, far, weights, sib, model)
    distant, peer[0] = lax.optimization_barrier((distant, peer[0]))
    over = move(distant, far_flip, 2)
    over, outs = lax.optimization_barrier((over, average(0, ())))
    projected = place_blocks(place, ((near, 0), (near, 1), (over, 0), (over, 1)))
    peer[1], projected = lax.optimization_barrier((peer[1], projected))
    return (projected, *average(1, outs))


def local(tokens, gain, weight, momentum, key_grad, step):
    rate = 0.05 + 0.1 * step.astype(jnp.float32) / 1000.0
    reps, shards = lax.axis_size("rep"), lax.axis_size("fsdp")
    levels = min(5, reps.bit_length() - 1)
    place = lax.axis_index("fsdp").reshape(1)
    branches = [partial(branch, bit, reps, shards) for bit in range(levels)]
    outs = lax.switch(
        lax.rem(step[0], levels),
        branches,
        tokens[0],
        gain,
        weight[0],
        momentum[0],
        key_grad[0],
        place,
        rate,
        step[0] >= 0,
    )
    return tuple(out[None] for out in outs)


def solution(mesh):
    split = P("rep", "fsdp", None)
    return jax.shard_map(
        local,
        mesh=mesh,
        in_specs=(split, P("rep", None), split, split, split, P()),
        out_specs=(split, split, split),
        check_vma=False,
    )
```

```python
from functools import partial

import jax
import jax.numpy as jnp
from jax import lax
from jax.experimental import pallas as pl
from jax.experimental.pallas import tpu as pltpu
from jax.sharding import PartitionSpec as P

epsilon = 1e-05
moment_decay = 0.9
AXES = ("rep", "fsdp")
PARTS = 2


def norm_kernel(place, tok, gains, k_far, k_cross, *parts):
    rows, model = tok.shape
    width = model // len(parts)
    block = k_far.shape[1]
    step, piece = 16, 512

    @pl.loop(0, rows // step)
    def _(i):
        at = pl.ds(pl.multiple_of(i * step, step), step)
        squares = jnp.zeros((step, piece), jnp.float32)
        for c in range(0, model, piece):
            values = tok[at, c : c + piece].astype(jnp.float32)
            squares += values * values
        inverse = lax.rsqrt(jnp.sum(squares, axis=-1, keepdims=True) / model + epsilon)
        for c in range(0, model, piece):
            values = tok[at, c : c + piece].astype(jnp.float32)
            normed = (values * inverse * gains[:, c : c + piece]).astype(jnp.bfloat16)
            parts[c // width][at, c % width : c % width + piece] = normed

    parts[0][:, width : width + block] = k_far[...]
    parts[0][:, width + block :] = k_cross[...]


def normalize(tok, gains, grads, place):
    rows, model = tok.shape
    block = grads.shape[1] // 4
    step = 64
    widths = [model // PARTS + (2 * block if i == 0 else 0) for i in range(PARTS)]

    def k_spec(flip):
        return pl.BlockSpec((step, block), lambda i, p: (i, p[0] ^ flip))

    return pl.pallas_call(
        norm_kernel,
        grid_spec=pltpu.PrefetchScalarGridSpec(
            num_scalar_prefetch=1,
            grid=(rows // step,),
            in_specs=[
                pl.BlockSpec((step, model), lambda i, p: (i, 0)),
                pl.BlockSpec((1, model), lambda i, p: (0, 0)),
                k_spec(2),
                k_spec(3),
            ],
            out_specs=[pl.BlockSpec((step, w), lambda i, p: (i, 0)) for w in widths],
        ),
        out_shape=[jax.ShapeDtypeStruct((rows, w), jnp.bfloat16) for w in widths],
        cost_estimate=pl.CostEstimate(
            flops=4 * rows * model, bytes_accessed=5 * rows * model, transcendentals=rows
        ),
        name="normalize",
    )(place, tok, gains, grads, grads)


def pack_kernel(place, *refs):
    *parts, weights, grads, whole, held, sems = refs
    width, model = weights.shape[1] // len(parts), weights.shape[1]
    block = grads.shape[1] // 4
    keys = pl.ds(pl.multiple_of((place[0] ^ 1) * block, block), block)
    pieces = [(part.at[:, :width], p * width, width) for p, part in enumerate(parts)]
    pieces += [(weights, model, model), (grads.at[:, keys], 2 * model, block)]
    copies = [
        pltpu.make_async_copy(ref, held.at[:, at : at + size], sems.at[i])
        for i, (ref, at, size) in enumerate(pieces)
    ]
    for copy in copies:
        copy.start()
    for copy in copies:
        copy.wait()
    out = pltpu.make_async_copy(held, whole, sems.at[len(copies)])
    out.start()
    out.wait()


def pack(parts, weights, grads, place):
    rows, model = weights.shape
    shape = (rows, 2 * model + grads.shape[1] // 4)
    hbm = pl.BlockSpec(memory_space=pltpu.HBM)
    return pl.pallas_call(
        pack_kernel,
        in_specs=[pl.BlockSpec(memory_space=pltpu.SMEM)] + [hbm] * (len(parts) + 2),
        out_specs=hbm,
        out_shape=jax.ShapeDtypeStruct(shape, jnp.bfloat16),
        scratch_shapes=[pltpu.VMEM(shape, jnp.bfloat16), pltpu.SemaphoreType.DMA((len(parts) + 3,))],
        compiler_params=pltpu.CompilerParams(vmem_limit_bytes=16 << 20),
        cost_estimate=pl.CostEstimate(flops=0, bytes_accessed=4 * shape[0] * shape[1], transcendentals=0),
        name="pack",
    )(place, *parts, weights, grads)


def moment_kernel(scale, piece, place, k_own, k_sib, k_far, k_cross, n_own, n_sib, n_far, n_cross, moments, new, sent, keys, turned):
    @pl.when(pl.program_id(0) == 0)
    def _():
        @pl.loop(0, k_own.shape[0] // 32)
        def _(i):
            at = pl.ds(pl.multiple_of(i * 32, 32), 32)
            for s, k in enumerate((k_own, k_sib, k_far, k_cross)):
                keys[s, at, :] = k[at, :]

        @pl.loop(0, 4)
        def _(s):
            turned[s] = keys[s].T

    @pl.loop(0, new.shape[1] // piece)
    def _(i):
        at = pl.ds(pl.multiple_of(i * piece, piece), piece)
        total = None
        for s, n in enumerate((n_own, n_sib, n_far, n_cross)):
            product = jnp.dot(turned[s], n[:, at], preferred_element_type=jnp.float32)
            total = product if total is None else total + product
        value = moment_decay * moments[:, at].astype(jnp.float32) + total * scale
        new[:, at] = value
        sent[:, at] = value.astype(jnp.bfloat16)


def moment_part(scale, place, grads, own, sib, far, cross, first, moments, start, columns):
    rows, model = moments.shape
    tokens = own.shape[0]
    tile = 1024
    k_specs = [
        pl.BlockSpec((tokens, rows), lambda i, p: (0, p[0])),
        pl.BlockSpec((tokens, rows), lambda i, p: (0, 2 * model // rows)),
        pl.BlockSpec((tokens, rows), lambda i, p: (0, columns // rows)),
        pl.BlockSpec((tokens, rows), lambda i, p: (0, columns // rows + 1)),
    ]
    whole_spec = pl.BlockSpec((tokens, tile), lambda i, p: (0, start // tile + i))
    part_spec = pl.BlockSpec((tokens, tile), lambda i, p: (0, i))
    m_spec = pl.BlockSpec((rows, tile), lambda i, p: (0, start // tile + i))
    o_spec = pl.BlockSpec((rows, tile), lambda i, p: (0, i))
    return pl.pallas_call(
        partial(moment_kernel, scale, 256),
        grid_spec=pltpu.PrefetchScalarGridSpec(
            num_scalar_prefetch=1,
            grid=(columns // tile,),
            in_specs=k_specs + [whole_spec] * 2 + [part_spec] * 2 + [m_spec],
            out_specs=[o_spec, o_spec],
            scratch_shapes=[
                pltpu.VMEM((4, tokens, rows), jnp.bfloat16),
                pltpu.VMEM((4, rows, tokens), jnp.bfloat16),
            ],
        ),
        out_shape=[
            jax.ShapeDtypeStruct((rows, columns), jnp.float32),
            jax.ShapeDtypeStruct((rows, columns), jnp.bfloat16),
        ],
        cost_estimate=pl.CostEstimate(
            flops=8 * tokens * rows * columns,
            bytes_accessed=(8 * tokens + 8 * rows) * columns,
            transcendentals=0,
        ),
        name="moment_part",
    )(place, grads, sib, *first, own, sib, far, cross, moments)


def project_kernel(scale, per, *refs):
    *sources, own, other, out, total = refs
    i = pl.program_id(0)
    rows = own.shape[0]

    piece, step = 256, 32

    @pl.when(i == 0)
    def _():
        @pl.loop(0, total.shape[0] // step)
        def _(r):
            at = pl.ds(pl.multiple_of(r * step, step), step)
            total[at, :] = jnp.zeros((step, total.shape[1]), jnp.float32)

    for part, source in enumerate(sources):

        @pl.when(i // per == part)
        def _(source=source):
            @pl.loop(0, own.shape[1] // piece)
            def _(c):
                at = pl.ds(pl.multiple_of(c * piece, piece), piece)
                for g, weights in enumerate((own, other)):
                    total[:, g * rows : (g + 1) * rows] += lax.dot_general(
                        source[:, at],
                        weights[:, at],
                        (((1,), (1,)), ((), ())),
                        preferred_element_type=jnp.float32,
                    )

    @pl.when(i == pl.num_programs(0) - 1)
    def _():
        @pl.loop(0, total.shape[0] // step)
        def _(r):
            at = pl.ds(pl.multiple_of(r * step, step), step)
            out[at, :] = (total[at, :] * scale).astype(jnp.bfloat16)


def project(scale, parts, own, other, offset):
    tokens = parts[0].shape[0]
    rows, model = own.shape
    tile = 512
    tiles = model // tile
    per = tiles // len(parts)
    n_specs = [
        pl.BlockSpec((tokens, tile), lambda i, part=part: (0, jnp.clip(i - part * per, 0, per - 1)))
        for part in range(len(parts))
    ]
    return pl.pallas_call(
        partial(project_kernel, scale, per),
        grid=(tiles,),
        in_specs=n_specs
        + [pl.BlockSpec((rows, tile), lambda i, at=at: (0, at // tile + i)) for at in (0, offset)],
        out_specs=pl.BlockSpec((tokens, 2 * rows), lambda i: (0, 0)),
        out_shape=jax.ShapeDtypeStruct((tokens, 2 * rows), jnp.bfloat16),
        scratch_shapes=[pltpu.VMEM((tokens, 2 * rows), jnp.float32)],
        cost_estimate=pl.CostEstimate(
            flops=4 * tokens * rows * model,
            bytes_accessed=(2 * tokens + 4 * rows) * model,
            transcendentals=0,
        ),
        name="project",
    )(*parts, own, other)


def place_kernel(place, *refs):
    *blocks, out = refs
    for k, block in enumerate(blocks):

        @pl.when(pl.program_id(0) == k)
        def _(block=block):
            @pl.loop(0, block.shape[0] // 32)
            def _(i):
                at = pl.ds(pl.multiple_of(i * 32, 32), 32)
                out[at, :] = block[at, :]


def place_blocks(place, blocks):
    rows, columns = blocks[0][0].shape
    width = columns // 2
    count = len(blocks)
    return pl.pallas_call(
        place_kernel,
        grid_spec=pltpu.PrefetchScalarGridSpec(
            num_scalar_prefetch=1,
            grid=(count,),
            in_specs=[pl.BlockSpec((rows, width), lambda i, p, half=half: (0, half)) for _, half in blocks],
            out_specs=pl.BlockSpec((rows, width), lambda i, p: (0, p[0] ^ i)),
        ),
        out_shape=jax.ShapeDtypeStruct((rows, count * width), jnp.bfloat16),
        cost_estimate=pl.CostEstimate(
            flops=0, bytes_accessed=4 * count * rows * width, transcendentals=0
        ),
        name="place_blocks",
    )(place, *[block for block, _ in blocks])


def average_kernel(start, rate, new, peer, weights, peer_weights, *refs):
    weight_out, moment_out, n_buf, p_buf, w_buf, q_buf, wo_buf, mo_buf, in_sems, out_sems = refs[-10:]
    tiles, rows, tile = n_buf.shape
    step = 128

    def columns(t, start):
        return pl.ds(pl.multiple_of(start + t * tile, tile), tile)

    def takes(t):
        pairs = ((new, 0, n_buf), (peer, 0, p_buf), (weights, start, w_buf), (peer_weights, start, q_buf))
        return [
            pltpu.make_async_copy(ref.at[:, columns(t, at)], buf.at[t], in_sems.at[t, i])
            for i, (ref, at, buf) in enumerate(pairs)
        ]

    def gives(t):
        return [
            pltpu.make_async_copy(buf.at[t], ref.at[:, columns(t, start)], out_sems.at[t, i])
            for i, (buf, ref) in enumerate(((wo_buf, weight_out), (mo_buf, moment_out)))
        ]

    @pl.loop(0, tiles)
    def _(t):
        for copy in takes(t):
            copy.start()

    @pl.loop(0, tiles)
    def _(t):
        for copy in takes(t):
            copy.wait()

        @pl.loop(0, rows // step)
        def _(i):
            at = pl.ds(pl.multiple_of(i * step, step), step)
            moment = (n_buf[t, at, :] + p_buf[t, at, :].astype(jnp.float32)) * 0.5
            weight = w_buf[t, at, :].astype(jnp.float32) + q_buf[t, at, :].astype(jnp.float32)
            wo_buf[t, at, :] = (weight * 0.5 - rate[0] * moment).astype(jnp.bfloat16)
            mo_buf[t, at, :] = moment.astype(jnp.bfloat16)

        for copy in gives(t):
            copy.start()

    @pl.loop(0, tiles)
    def _(t):
        for copy in gives(t):
            copy.wait()


def average_part(rate, new, peer, weights, peer_weights, start, outs):
    rows, model = weights.shape
    columns = new.shape[1]
    tile = 512
    tiles = columns // tile
    hbm = pl.BlockSpec(memory_space=pltpu.HBM)
    shape = jax.ShapeDtypeStruct((rows, model), jnp.bfloat16)
    buf = pltpu.VMEM((tiles, rows, tile), jnp.bfloat16)
    return pl.pallas_call(
        partial(average_kernel, start),
        in_specs=[pl.BlockSpec(memory_space=pltpu.SMEM)] + [hbm] * (4 + len(outs)),
        out_specs=[hbm, hbm],
        out_shape=[shape, shape],
        input_output_aliases={5 + i: i for i in range(len(outs))},
        scratch_shapes=[
            pltpu.VMEM((tiles, rows, tile), jnp.float32),
            *[buf] * 5,
            pltpu.SemaphoreType.DMA((tiles, 4)),
            pltpu.SemaphoreType.DMA((tiles, 2)),
        ],
        compiler_params=pltpu.CompilerParams(vmem_limit_bytes=24 << 20),
        cost_estimate=pl.CostEstimate(
            flops=6 * rows * columns, bytes_accessed=14 * rows * columns, transcendentals=0
        ),
        name="average_part",
    )(rate, new, peer, weights, peer_weights, *outs)


def stage(always, work, *operands):
    def idle(*operands):
        outs, tree = jax.tree.flatten(jax.eval_shape(work, *operands))
        blank = pl.pallas_call(
            lambda *refs: None,
            out_specs=[pl.BlockSpec(memory_space=pltpu.HBM)] * len(outs),
            out_shape=[jax.ShapeDtypeStruct(out.shape, out.dtype) for out in outs],
            name="blank",
        )()
        return jax.tree.unflatten(tree, blank)

    return lax.cond(always, work, idle, *operands)


def branch(bit, reps, shards, tok, gains, weights, moments, grads, place, rate, always):
    model = tok.shape[1]
    scale = float(model) ** (-0.5)
    rows = weights.shape[0]
    columns = model // PARTS
    low_bit = 2

    def move(value, rep_flip, shard_flip):
        pairs = [
            (r * shards + s, (r ^ rep_flip) * shards + (s ^ shard_flip))
            for r in range(reps)
            for s in range(shards)
        ]
        return lax.ppermute(value, AXES, pairs)

    flip = 1 << bit
    far_flip = flip if bit == low_bit else 0

    peer_weights = move(weights, flip, 0)
    own_parts = normalize(tok, gains, grads, place)
    far = [move(part, far_flip, 2) for part in own_parts]

    def near_stage(parts, weights, grads):
        own = pack(parts, weights, grads, place)
        sib = move(own, 0, 1)
        return own, sib, project(scale, [own], weights, sib, model)

    own, sib, near = stage(always, near_stage, own_parts, weights, grads)
    far[0], near = lax.optimization_barrier((far[0], near))

    def moment_stage(part, own, sib, here, first, grads, moments, share):
        there = move(here, 0, 1)
        shared = [move(value, 0, 1) for value in share]
        first = (here, there) if first is None else first
        new, sent = moment_part(
            scale, place, grads, own, sib, here, there, first, moments, part * columns, columns
        )
        return new, sent, there, shared

    new, peer, cross, sent, shared = [], [], [], None, []
    for part in range(PARTS):
        if part:
            far[part], sent = lax.optimization_barrier((far[part], sent))
        first = (far[0], cross[0]) if part else None
        share = [peer_weights] if part and far_flip else []
        value, sent, there, shared = stage(
            always, partial(moment_stage, part), own, sib, far[part], first, grads, moments, share
        )
        new.append(value)
        cross.append(there)
        if part == 0:
            sent, peer_weights = lax.optimization_barrier((sent, peer_weights))
        peer.append(move(sent, flip, 0))

    def average(part, outs):
        return average_part(rate, new[part], peer[part], weights, peer_weights, part * columns, outs)

    far[0], _ = lax.optimization_barrier((far[0], sent))
    if far_flip:
        distant = project(scale, far, peer_weights, shared[0], 0)
    else:
        distant = project(scale, far, weights, sib, model)
    distant, peer[0] = lax.optimization_barrier((distant, peer[0]))
    over = move(distant, far_flip, 2)
    over, outs = lax.optimization_barrier((over, average(0, ())))
    projected = place_blocks(place, ((near, 0), (near, 1), (over, 0), (over, 1)))
    peer[1], projected = lax.optimization_barrier((peer[1], projected))
    return (projected, *average(1, outs))


def local(tokens, gain, weight, momentum, key_grad, step):
    rate = 0.05 + 0.1 * step.astype(jnp.float32) / 1000.0
    reps, shards = lax.axis_size("rep"), lax.axis_size("fsdp")
    levels = min(5, reps.bit_length() - 1)
    place = lax.axis_index("fsdp").reshape(1)
    branches = [partial(branch, bit, reps, shards) for bit in range(levels)]
    outs = lax.switch(
        lax.rem(step[0], levels),
        branches,
        tokens[0],
        gain,
        weight[0],
        momentum[0],
        key_grad[0],
        place,
        rate,
        step[0] >= 0,
    )
    return tuple(out[None] for out in outs)


def solution(mesh):
    split = P("rep", "fsdp", None)
    return jax.shard_map(
        local,
        mesh=mesh,
        in_specs=(split, P("rep", None), split, split, split, P()),
        out_specs=(split, split, split),
        check_vma=False,
    )
```
